128 devices in a mesh: section: 2 (over z_lo), dp: 8 (over y, core), tensor: 8 (over z_hi, x).
Axes of the slice: x: 4, y: 4, z: 4 (z_hi: 2, z_lo: 2; z = z_hi * 2 + z_lo), core: 2. Of those that a mesh axis runs over, the one named last changes fastest.
Arguments:
- inputs: bfloat16 [384, 8192], P('tensor', 'dp'), may hold values from -6 to 6
- cotangent: bfloat16 [384, 8192], P('tensor', 'dp'), may hold values from -1.5 to 1.5
- gate_weight: bfloat16 [2, 8192, 14336], P('section', 'dp', 'tensor'), may hold values from -0.0625 to 0.0625
- up_weight: bfloat16 [2, 8192, 14336], P('section', 'dp', 'tensor'), may hold values from -0.0625 to 0.0625
- down_weight: bfloat16 [2, 14336, 8192], P('section', 'tensor', 'dp'), may hold values from -0.046875 to 0.046875
Outputs:
- section_out: bfloat16 [2, 384, 8192], P('section', 'tensor', 'dp')
- input_grad: bfloat16 [2, 384, 8192], P('section', 'tensor', 'dp')
- gate_grad: bfloat16 [2, 8192, 14336], P('section', 'dp', 'tensor')
- up_grad: bfloat16 [2, 8192, 14336], P('section', 'dp', 'tensor')
- down_grad: bfloat16 [2, 14336, 8192], P('section', 'tensor', 'dp')
The draws below stay inside these ranges and needn't reach their ends.
All inputs are finite; a program needn't handle non-finite values.
Results may differ from the reference program's by a relative error of at most 0.015.
Values may be sent and summed in bfloat16 or wider, within the bound.
A program may use at most 128 MiB of HBM per device.

```python
import jax
import jax.numpy as jnp

D = 8192
FF = 14336
TOKENS = 384


def block_levels(stream_key, dims, cuts, low, top_value):
    factor_of = 1.0
    for position, parts in cuts:
        heights = jax.random.uniform(jax.random.fold_in(jax.random.fold_in(stream_key, 6), position), (parts,), jnp.float32, low / len(cuts), top_value / len(cuts))
        factor_of = factor_of * jnp.repeat(jnp.exp(heights), dims[position] // parts).reshape((-1,) + (1,) * (len(dims) - 1 - position))
    return factor_of


def noise(key, shape, deviation, most, pieces=(), dtype=jnp.bfloat16):
    drawn = deviation * jax.random.normal(key, shape, jnp.float32)
    if pieces:
        drawn = drawn * block_levels(key, shape, pieces, -0.22, 0.18)
    return jnp.clip(drawn, -most, most).astype(dtype)


def setup_inputs(seed: int = 0) -> dict:
    key_list = jax.random.split(jax.random.key(seed), 6)
    return {
        "inputs": noise(key_list[0], (TOKENS, D), 1.0, 6.0, ((0, 8), (1, 8))),
        "cotangent": noise(key_list[1], (TOKENS, D), 0.25, 1.5, ((0, 8), (1, 8))),
        "gate_weight": noise(key_list[2], (2, D, FF), D ** -0.5, 0.0625, ((0, 2), (1, 8), (2, 8))),
        "up_weight": noise(key_list[3], (2, D, FF), D ** -0.5, 0.0625, ((0, 2), (1, 8), (2, 8))),
        "down_weight": noise(key_list[4], (2, FF, D), FF ** -0.5, 0.046875, ((0, 2), (1, 8), (2, 8))),
    }


def layer_forward(layer_in, w_gate, w_up, w_down):
    gate_pre = jnp.dot(layer_in, w_gate, preferred_element_type=jnp.float32)
    up_pre = jnp.dot(layer_in, w_up, preferred_element_type=jnp.float32)
    hidden = (jax.nn.silu(gate_pre) * up_pre).astype(jnp.bfloat16)
    summed = jnp.dot(hidden, w_down, preferred_element_type=jnp.float32)
    layer_out = (layer_in.astype(jnp.float32) + summed).astype(jnp.bfloat16)
    return layer_out, gate_pre, up_pre, hidden


def layer_backward(layer_in, grad_out, gate_pre, up_pre, hidden, w_gate, w_up, w_down):
    grad_hidden = jnp.dot(grad_out, w_down.T, preferred_element_type=jnp.float32)
    down_part = jnp.dot(hidden.T, grad_out, preferred_element_type=jnp.float32).astype(jnp.bfloat16)
    sigma = jax.nn.sigmoid(gate_pre)
    grad_gate = (grad_hidden * up_pre * sigma * (1.0 + gate_pre * (1.0 - sigma))).astype(jnp.bfloat16)
    grad_up = (grad_hidden * gate_pre * sigma).astype(jnp.bfloat16)
    gate_part = jnp.dot(layer_in.T, grad_gate, preferred_element_type=jnp.float32).astype(jnp.bfloat16)
    up_part = jnp.dot(layer_in.T, grad_up, preferred_element_type=jnp.float32).astype(jnp.bfloat16)
    back_sum = jnp.dot(grad_gate, w_gate.T, preferred_element_type=jnp.float32) + jnp.dot(grad_up, w_up.T, preferred_element_type=jnp.float32)
    grad_in = (grad_out.astype(jnp.float32) + back_sum).astype(jnp.bfloat16)
    return grad_in, gate_part, up_part, down_part


def reference(inputs, cotangent, gate_weight, up_weight, down_weight):
    first_out, gate_first, up_first, hidden_first = layer_forward(inputs, gate_weight[0], up_weight[0], down_weight[0])
    second_out, gate_second, up_second, hidden_second = layer_forward(first_out, gate_weight[1], up_weight[1], down_weight[1])
    grad_mid, gate_two, up_two, down_two = layer_backward(first_out, cotangent, gate_second, up_second, hidden_second, gate_weight[1], up_weight[1], down_weight[1])
    grad_start, gate_one, up_one, down_one = layer_backward(inputs, grad_mid, gate_first, up_first, hidden_first, gate_weight[0], up_weight[0], down_weight[0])
    section_out = jnp.stack([first_out, second_out])
    input_grad = jnp.stack([grad_start, grad_mid])
    return (section_out, input_grad, jnp.stack([gate_one, gate_two]), jnp.stack([up_one, up_two]), jnp.stack([down_one, down_two]))
```

```python
import jax
import jax.numpy as jnp
from jax import lax
from jax.experimental import pallas as pl
from jax.experimental.pallas import tpu as pltpu
from jax.sharding import PartitionSpec as P

MESH = pl.DeviceIdType.MESH
F32 = jnp.float32
BF16 = jnp.bfloat16

D = 1024
HID = 1792
HC = HID // 2
TB = 48
HT = 4 * TB

BUFFERS = {
    "wg": ((D, HID), BF16),
    "wu": ((D, HID), BF16),
    "wd": ((HID, D), BF16),
    "u": ((2, 4, TB, D), BF16),
    "g": ((2, 4, TB, D), BF16),
    "hid": ((2, 4, TB, HID), BF16),
    "grad": ((2, 4, 2, TB, HID), BF16),
    "fac": ((2, 4, 2, TB, HID), BF16),
    "gh": ((2, 4, TB, HID), BF16),
    "f_psend": ((2, 2, 4, TB, HC), BF16),
    "f_precv": ((2, 2, 4, TB, HC), BF16),
    "f_own": ((2, 2, 4, TB, HC), F32),
    "f_ysend": ((2, 3, 2, TB, HC), BF16),
    "f_yrecv": ((2, 3, 2, TB, HC), BF16),
    "b_psend": ((2, 1, 4, TB, HC), BF16),
    "b_precv": ((2, 1, 4, TB, HC), BF16),
    "b_own": ((2, 1, 4, TB, HC), F32),
    "b_ysend": ((2, 3, 1, TB, HC), BF16),
    "b_yrecv": ((2, 3, 1, TB, HC), BF16),
    "ghown": ((2, TB, HC), F32),
    "xsend": ((2, 2, 4, TB, D), BF16),
    "xown": ((2, 2, 4, TB, D), F32),
    "xrecv": ((2, 2, 3, TB, D), BF16),
    "zsend": ((2, TB, D), BF16),
    "zrecv": ((2, 2, TB, D), BF16),
    "home": ((TB, D), BF16),
    "zzsend": ((TB, D), BF16),
    "zzrecv": ((TB, D), BF16),
    "og": ((D, HID), BF16),
    "ou": ((D, HID), BF16),
    "od": ((HID, D), BF16),
}


def slot_table():
    names = []
    names += [("near", 0, k) for k in (1, 2, 3)] + [("cross", 0, k) for k in range(4)]
    for h in range(2):
        for p in ("f", "b"):
            names.append((p + "pair", h))
            names += [(p + "y", h, k) for k in (1, 2, 3)]
        for a in ("hid", "grad", "fac", "gh"):
            names += [(a + "y", h, k) for k in (1, 2, 3)]
            names += [(a + "p", h, k) for k in range(4)]
        for tag in range(2):
            names += [("x", tag, h, k) for k in (1, 2, 3)]
        names += [("z", h, 0), ("z", h, 1)]
        names += [("xg", h, k) for k in (1, 2, 3)]
    names += [("home",), ("zz",)]
    return {name: i for i, name in enumerate(names)}


SLOTS = slot_table()


def tiles(total, width=256):
    return [(o, min(width, total - o)) for o in range(0, total, width)]


def dot_nn(a, b):
    return lax.dot_general(a, b, (((1,), (0,)), ((), ())), preferred_element_type=F32)


def dot_nt(a, b):
    return lax.dot_general(a, b, (((1,), (1,)), ((), ())), preferred_element_type=F32)


def dot_tn(a, b):
    return lax.dot_general(a, b, (((0,), (0,)), ((), ())), preferred_element_type=F32)


def kernel(in_ref, ct_ref, wg_hbm, wu_hbm, wd_hbm, so_ref, ig_ref, og_hbm, ou_hbm, od_hbm, *scratch):
    b = dict(zip(BUFFERS, scratch))
    send_sem, recv_sem, load_sem, out_sem = scratch[len(BUFFERS):]
    s, d, t = lax.axis_index("section"), lax.axis_index("dp"), lax.axis_index("tensor")
    y, c = d // 2, d % 2
    zh, x = t // 4, t % 4

    def ring(v, k):
        return (v + k) % 4

    def at_y(k):
        return {"dp": ring(y, k) * 2 + c}

    def at_x(k):
        return {"tensor": zh * 4 + ring(x, k)}

    def at_cross(k):
        return {"section": 1 - s, "tensor": (1 - zh) * 4 + ring(x, k)}

    def at_other(z):
        return {"section": 1 - s, "tensor": z * 4 + x}

    pair = {"dp": y * 2 + 1 - c}
    zz_peer = {"tensor": (1 - zh) * 4 + x}
    same = {"section": 1 - s}
    col = pl.multiple_of(c * HC, 128)
    col_other = pl.multiple_of((1 - c) * HC, 128)

    weights = {}
    for i, (name, src) in enumerate((("wg", wg_hbm), ("wu", wu_hbm), ("wd", wd_hbm))):
        weights[name] = pltpu.make_async_copy(src, b[name], load_sem.at[i])
        weights[name].start()

    barrier = pltpu.get_barrier_semaphore()
    peers = [pair, zz_peer, same]
    peers += [at_y(k) for k in (1, 2, 3)] + [at_x(k) for k in (1, 2, 3)]
    peers += [at_cross(k) for k in range(4)]
    for peer in peers:
        pl.semaphore_signal(barrier, 1, device_id=peer, device_id_type=MESH)
    pl.semaphore_wait(barrier, len(peers))

    def role(first):
        sent = []
        outs = []

        def send(slot, src, dst, peer):
            i = SLOTS[slot]
            copy = pltpu.make_async_remote_copy(
                src_ref=src, dst_ref=dst, send_sem=send_sem.at[i], recv_sem=recv_sem.at[i],
                device_id=peer, device_id_type=MESH,
            )
            copy.start()
            sent.append(copy)

        def arrived(slot, dst):
            i = SLOTS[slot]
            pltpu.make_async_remote_copy(
                src_ref=dst, dst_ref=dst, send_sem=send_sem.at[i], recv_sem=recv_sem.at[i],
                device_id=pair, device_id_type=MESH,
            ).wait_recv()

        mine, theirs = (in_ref, ct_ref) if first else (ct_ref, in_ref)
        full, full_there = (b["u"], b["g"]) if first else (b["g"], b["u"])

        def send_near():
            for k in (2, 1, 3):
                send(("near", 0, k), mine, full.at[zh, x], at_x(k))

        def send_cross():
            for k in (2, 1, 3, 0):
                send(("cross", 0, k), theirs, full_there.at[zh, x], at_cross(k))

        def gather_wait():
            for k in (1, 2, 3):
                arrived(("near", 0, k), full.at[zh, ring(x, 4 - k)])
            for k in range(4):
                arrived(("cross", 0, k), full.at[1 - zh, ring(x, 4 - k)])

        def mm_forward(h):
            u = b["u"][h].reshape(HT, D)
            for dst, start in ((b["f_psend"], col_other), (b["f_own"], col)):
                for a, w in enumerate((b["wg"], b["wu"])):
                    for o, n in tiles(HC):
                        r = dot_nn(u, w[:, pl.ds(pl.multiple_of(start + o, 128), n)])
                        dst[h, a, :, :, o:o + n] = r.reshape(4, TB, n).astype(dst.dtype)
                if dst is b["f_psend"]:
                    send(("fpair", h), dst.at[h], b["f_precv"].at[h], pair)

        def mm_hidden(h):
            g = b["g"][h].reshape(HT, D)
            for dst, start in ((b["b_psend"], col_other), (b["b_own"], col)):
                for o, n in tiles(HC):
                    r = dot_nt(g, b["wd"][pl.ds(pl.multiple_of(start + o, 128), n), :])
                    dst[h, 0, :, :, o:o + n] = r.reshape(4, TB, n).astype(dst.dtype)
                if dst is b["b_psend"]:
                    send(("bpair", h), dst.at[h], b["b_precv"].at[h], pair)

        def pair_add(p, h):
            own, prec, ysend, yrecv = (b[p + n] for n in ("_own", "_precv", "_ysend", "_yrecv"))
            arrived((p + "pair", h), prec.at[h])
            for k in (2, 1, 3):
                j = ring(y, k)
                for a in range(own.shape[1]):
                    ysend[h, k - 1, a] = (own[h, a, j] + prec[h, a, j].astype(F32)).astype(BF16)
                send((p + "y", h, k), ysend.at[h, k - 1], yrecv.at[h, k - 1], at_y(k))

        def y_sum(p, h):
            own, prec, yrecv = (b[p + n] for n in ("_own", "_precv", "_yrecv"))
            total = [own[h, a, y] + prec[h, a, y].astype(F32) for a in range(own.shape[1])]
            for k in (1, 3, 2):
                arrived((p + "y", h, k), yrecv.at[h, k - 1])
            for k in (1, 2, 3):
                total = [v + yrecv[h, k - 1, a].astype(F32) for a, v in enumerate(total)]
            return total

        def block(name, h, j, start):
            ref = b[name]
            cols = pl.ds(start, HC)
            return ref.at[h, j, :, :, cols] if len(ref.shape) == 5 else ref.at[h, j, :, cols]

        def spread(name, h):
            ref = block(name, h, y, col)
            for k in (2, 1, 3):
                send((name + "y", h, k), ref, ref, at_y(k))
            send((name + "p", h, 0), ref, ref, pair)

        def forward_pair(name, h):
            for k in (1, 3, 2):
                ref = block(name, h, ring(y, 4 - k), col)
                arrived((name + "y", h, k), ref)
                send((name + "p", h, k), ref, ref, pair)

        def pair_wait(name, h):
            for k in (0, 1, 3, 2):
                arrived((name + "p", h, k), block(name, h, ring(y, 4 - k), col_other))

        def x_scatter(tag, h, term):
            for o, n in tiles(D):
                r = term(o, n).reshape(4, TB, n)
                b["xown"][tag, h, :, :, o:o + n] = r
                b["xsend"][tag, h, :, :, o:o + n] = r.astype(BF16)
            for k in (2, 1, 3):
                send(("x", tag, h, k), b["xsend"].at[tag, h, ring(x, k)], b["xrecv"].at[tag, h, k - 1], at_x(k))

        def x_sum(tag, h):
            for k in (1, 3, 2):
                arrived(("x", tag, h, k), b["xrecv"].at[tag, h, k - 1])
            total = b["xown"][tag, h, x]
            for k in (1, 2, 3):
                total = total + b["xrecv"][tag, h, k - 1].astype(F32)
            return total

        def down(tag, h):
            hid = b["hid"][h].reshape(HT, HID)
            x_scatter(tag, h, lambda o, n: dot_nn(hid, b["wd"][:, o:o + n]))

        def back(tag, h):
            gg = b["grad"][h, :, 0].reshape(HT, HID)
            gu = b["grad"][h, :, 1].reshape(HT, HID)
            x_scatter(tag, h, lambda o, n: dot_nt(gg, b["wg"][o:o + n, :]) + dot_nt(gu, b["wu"][o:o + n, :]))

        def to_next(tag, h, residual):
            total = x_sum(tag, h) + jnp.where(zh == h, residual[...].astype(F32), 0.0)
            b["zsend"][h] = total.astype(BF16)
            send_z(h)

        def send_z(h):
            for z in range(2):
                i = SLOTS[("z", h, 0)] + zh
                copy = pltpu.make_async_remote_copy(
                    src_ref=b["zsend"].at[h], dst_ref=b["zrecv"].at[h, zh],
                    send_sem=send_sem.at[SLOTS[("z", h, z)]], recv_sem=recv_sem.at[i],
                    device_id=at_other(z), device_id_type=MESH,
                )
                copy.start()
                sent.append(copy)

        def from_other(h, dst):
            for z in range(2):
                arrived(("z", h, z), b["zrecv"].at[h, z])
            total = b["zrecv"][h, 0].astype(F32) + b["zrecv"][h, 1].astype(F32)
            dst[h, x] = total.astype(BF16)
            for k in (2, 1, 3):
                send(("xg", h, k), dst.at[h, x], dst.at[h, x], at_x(k))

        def x_gathered(h, dst):
            for k in (1, 3, 2):
                arrived(("xg", h, k), dst.at[h, ring(x, 4 - k)])

        def finish(tag, residual, out_ref):
            for h in range(2):
                b["xown"][tag, h, x] = x_sum(tag, h)
            b["zzsend"][...] = b["xown"][tag, 1 - zh, x].astype(BF16)
            send(("zz",), b["zzsend"], b["zzrecv"], zz_peer)

        def finish_wait(tag, residual, out_ref):
            arrived(("zz",), b["zzrecv"])
            total = b["xown"][tag, zh, x] + b["zzrecv"][...].astype(F32) + residual[zh, x].astype(F32)
            out_ref[0] = total.astype(BF16)

        def weight_grad(lhs, rhs, stage, out, i):
            for o, n in tiles(stage.shape[0]):
                stage[o:o + n, :] = dot_tn(lhs(o, n), rhs()).astype(BF16)
            copy = pltpu.make_async_copy(stage, out, out_sem.at[i])
            copy.start()
            outs.append(copy)

        def down_grad():
            weight_grad(
                lambda o, n: b["hid"][:, :, :, o:o + n].reshape(2 * HT, n),
                lambda: b["g"][...].reshape(2 * HT, D), b["od"], od_hbm, 2,
            )

        def gate_grad(a):
            weight_grad(
                lambda o, n: b["u"][:, :, :, o:o + n].reshape(2 * HT, n),
                lambda: b["grad"][:, :, a].reshape(2 * HT, HID),
                (b["og"], b["ou"])[a], (og_hbm, ou_hbm)[a], a,
            )

        both = range(2)
        if first:
            send_near()
            send_cross()
            full[zh, x] = in_ref[...]
            weights["wg"].wait()
            weights["wu"].wait()
            gather_wait()
            for h in both:
                mm_forward(h)
            for h in both:
                pair_add("f", h)
            for h in both:
                gate, up = y_sum("f", h)
                sig = 1.0 / (1.0 + jnp.exp(-gate))
                b["hid"][h, y, :, pl.ds(col, HC)] = (gate * sig * up).astype(BF16)
                spread("hid", h)
                b["fac"][h, y, 0, :, pl.ds(col, HC)] = (up * sig * (1.0 + gate * (1.0 - sig))).astype(BF16)
                b["fac"][h, y, 1, :, pl.ds(col, HC)] = (gate * sig).astype(BF16)
            weights["wd"].wait()
            for h in both:
                forward_pair("hid", h)
            for h in both:
                pair_wait("hid", h)
                down(0, h)
            for h in both:
                to_next(0, h, in_ref)
            for h in both:
                spread("fac", h)
            for h in both:
                forward_pair("fac", h)
            for h in both:
                pair_wait("fac", h)
            arrived(("home",), b["home"])
            so_ref[0] = b["home"][...]
            for h in both:
                from_other(h, b["g"])
            send(("home",), b["g"].at[zh, x], b["home"], same)
            for h in both:
                x_gathered(h, b["g"])
                mm_hidden(h)
            for h in both:
                pair_add("b", h)
            down_grad()
            for h in both:
                (gh,) = y_sum("b", h)
                b["gh"][h, y, :, pl.ds(col, HC)] = gh.astype(BF16)
                spread("gh", h)
            for h in both:
                forward_pair("gh", h)
            for h in both:
                pair_wait("gh", h)
                for j in range(4):
                    gh = b["gh"][h, j].astype(F32)
                    for a in range(2):
                        b["grad"][h, j, a] = (gh * b["fac"][h, j, a].astype(F32)).astype(BF16)
                back(1, h)
            gate_grad(0)
            finish(1, b["g"], ig_ref)
            gate_grad(1)
            finish_wait(1, b["g"], ig_ref)
        else:
            send_cross()
            send_near()
            full[zh, x] = ct_ref[...]
            weights["wd"].wait()
            gather_wait()
            for h in both:
                mm_hidden(h)
            for h in both:
                pair_add("b", h)
            for h in both:
                (b["ghown"][h],) = y_sum("b", h)
            weights["wg"].wait()
            weights["wu"].wait()
            for h in both:
                from_other(h, b["u"])
            send(("home",), b["u"].at[zh, x], b["home"], same)
            for h in both:
                x_gathered(h, b["u"])
                mm_forward(h)
            for h in both:
                pair_add("f", h)
            for h in both:
                gate, up = y_sum("f", h)
                sig = 1.0 / (1.0 + jnp.exp(-gate))
                gh = b["ghown"][h]
                grad_gate = gh * up * sig * (1.0 + gate * (1.0 - sig))
                b["grad"][h, y, 0, :, pl.ds(col, HC)] = grad_gate.astype(BF16)
                b["grad"][h, y, 1, :, pl.ds(col, HC)] = (gh * gate * sig).astype(BF16)
                spread("grad", h)
                b["hid"][h, y, :, pl.ds(col, HC)] = (gate * sig * up).astype(BF16)
            for h in both:
                forward_pair("grad", h)
            for h in both:
                pair_wait("grad", h)
                back(0, h)
            for h in both:
                to_next(0, h, ct_ref)
            for h in both:
                spread("hid", h)
            for h in both:
                forward_pair("hid", h)
            for h in both:
                pair_wait("hid", h)
                down(1, h)
            gate_grad(0)
            finish(1, b["u"], so_ref)
            gate_grad(1)
            down_grad()
            finish_wait(1, b["u"], so_ref)
            arrived(("home",), b["home"])
            ig_ref[0] = b["home"][...]
        for copy in sent:
            copy.wait_send()
        for copy in outs:
            copy.wait()

    pl.when(s == 0)(lambda: role(True))
    pl.when(s == 1)(lambda: role(False))


def per_device(inputs, cotangent, gate_weight, up_weight, down_weight):
    any_spec = pl.BlockSpec(memory_space=pl.ANY)
    vmem_spec = pl.BlockSpec(memory_space=pltpu.VMEM)
    n = len(SLOTS)
    outs = pl.pallas_call(
        kernel,
        out_shape=[
            jax.ShapeDtypeStruct((1, TB, D), BF16),
            jax.ShapeDtypeStruct((1, TB, D), BF16),
            jax.ShapeDtypeStruct((D, HID), BF16),
            jax.ShapeDtypeStruct((D, HID), BF16),
            jax.ShapeDtypeStruct((HID, D), BF16),
        ],
        in_specs=[vmem_spec, vmem_spec, any_spec, any_spec, any_spec],
        out_specs=[vmem_spec, vmem_spec, any_spec, any_spec, any_spec],
        scratch_shapes=[pltpu.VMEM(shape, dtype) for shape, dtype in BUFFERS.values()]
        + [
            pltpu.SemaphoreType.DMA((n,)),
            pltpu.SemaphoreType.DMA((n,)),
            pltpu.SemaphoreType.DMA((3,)),
            pltpu.SemaphoreType.DMA((3,)),
        ],
        compiler_params=pltpu.CompilerParams(
            collective_id=0, has_side_effects=True, vmem_limit_bytes=60 << 20
        ),
        name="sections",
    )(inputs, cotangent, gate_weight[0], up_weight[0], down_weight[0])
    return (outs[0], outs[1], outs[2][None], outs[3][None], outs[4][None])


def solution(mesh):
    in_specs = (
        P("tensor", "dp"),
        P("tensor", "dp"),
        P("section", "dp", "tensor"),
        P("section", "dp", "tensor"),
        P("section", "tensor", "dp"),
    )
    out_specs = (
        P("section", "tensor", "dp"),
        P("section", "tensor", "dp"),
        P("section", "dp", "tensor"),
        P("section", "dp", "tensor"),
        P("section", "tensor", "dp"),
    )
    return jax.shard_map(
        per_device, mesh=mesh, in_specs=in_specs, out_specs=out_specs, check_vma=False
    )
```

```python
import jax
import jax.numpy as jnp
from jax import lax
from jax.experimental import pallas as pl
from jax.experimental.pallas import tpu as pltpu
from jax.sharding import PartitionSpec as P

MESH = pl.DeviceIdType.MESH
F32 = jnp.float32
BF16 = jnp.bfloat16

D = 1024
HID = 1792
HC = HID // 2
TB = 48
HT = 4 * TB

BUFFERS = {
    "wg": ((D, HID), BF16),
    "wu": ((D, HID), BF16),
    "wd": ((HID, D), BF16),
    "u": ((2, 4, TB, D), BF16),
    "g": ((2, 4, TB, D), BF16),
    "hid": ((2, 4, TB, HID), BF16),
    "grad": ((2, 4, 2, TB, HID), BF16),
    "fac": ((2, 4, 2, TB, HID), BF16),
    "gh": ((2, 4, TB, HID), BF16),
    "f_psend": ((2, 2, 4, TB, HC), BF16),
    "f_precv": ((2, 2, 4, TB, HC), BF16),
    "f_own": ((2, 2, 4, TB, HC), F32),
    "f_ysend": ((2, 3, 2, TB, HC), BF16),
    "f_yrecv": ((2, 3, 2, TB, HC), BF16),
    "b_psend": ((2, 1, 4, TB, HC), BF16),
    "b_precv": ((2, 1, 4, TB, HC), BF16),
    "b_own": ((2, 1, 4, TB, HC), F32),
    "b_ysend": ((2, 3, 1, TB, HC), BF16),
    "b_yrecv": ((2, 3, 1, TB, HC), BF16),
    "ghown": ((2, TB, HC), F32),
    "xsend": ((2, 2, 4, TB, D), BF16),
    "xown": ((2, 2, 4, TB, D), F32),
    "xrecv": ((2, 2, 3, TB, D), BF16),
    "zsend": ((2, TB, D), BF16),
    "zrecv": ((2, 2, TB, D), BF16),
    "home": ((TB, D), BF16),
    "zzsend": ((TB, D), BF16),
    "zzrecv": ((TB, D), BF16),
}


def slot_table():
    names = []
    names += [("near", 0, k) for k in (1, 2, 3)] + [("cross", 0, k) for k in range(4)]
    for h in range(2):
        for p in ("f", "b"):
            names.append((p + "pair", h))
            names += [(p + "y", h, k) for k in (1, 2, 3)]
        for a in ("hid", "grad", "fac", "gh"):
            names += [(a + "y", h, k) for k in (1, 2, 3)]
            names += [(a + "p", h, k) for k in range(4)]
        for tag in range(2):
            names += [("x", tag, h, k) for k in (1, 2, 3)]
        names += [("z", h, 0), ("z", h, 1)]
        names += [("xg", h, k) for k in (1, 2, 3)]
    names += [("home",), ("zz",)]
    return {name: i for i, name in enumerate(names)}


SLOTS = slot_table()


def tiles(total, width=256):
    return [(o, min(width, total - o)) for o in range(0, total, width)]


def dot_nn(a, b):
    return lax.dot_general(a, b, (((1,), (0,)), ((), ())), preferred_element_type=F32)


def dot_nt(a, b):
    return lax.dot_general(a, b, (((1,), (1,)), ((), ())), preferred_element_type=F32)


def dot_tn(a, b):
    return lax.dot_general(a, b, (((0,), (0,)), ((), ())), preferred_element_type=F32)


def kernel(in_ref, ct_ref, wg_hbm, wu_hbm, wd_hbm, so_ref, ig_ref, og_ref, ou_ref, od_ref, *scratch):
    b = dict(zip(BUFFERS, scratch))
    send_sem, recv_sem, load_sem = scratch[len(BUFFERS):]
    s, d, t = lax.axis_index("section"), lax.axis_index("dp"), lax.axis_index("tensor")
    y, c = d // 2, d % 2
    zh, x = t // 4, t % 4

    def ring(v, k):
        return (v + k) % 4

    def at_y(k):
        return {"dp": ring(y, k) * 2 + c}

    def at_x(k):
        return {"tensor": zh * 4 + ring(x, k)}

    def at_cross(k):
        return {"section": 1 - s, "tensor": (1 - zh) * 4 + ring(x, k)}

    def at_other(z):
        return {"section": 1 - s, "tensor": z * 4 + x}

    pair = {"dp": y * 2 + 1 - c}
    zz_peer = {"tensor": (1 - zh) * 4 + x}
    same = {"section": 1 - s}
    col = pl.multiple_of(c * HC, 128)
    col_other = pl.multiple_of((1 - c) * HC, 128)

    weights = {}
    for i, (name, src) in enumerate((("wg", wg_hbm), ("wu", wu_hbm), ("wd", wd_hbm))):
        weights[name] = pltpu.make_async_copy(src.at[0], b[name], load_sem.at[i])
        weights[name].start()

    barrier = pltpu.get_barrier_semaphore()
    peers = [pair, zz_peer, same]
    peers += [at_y(k) for k in (1, 2, 3)] + [at_x(k) for k in (1, 2, 3)]
    peers += [at_cross(k) for k in range(4)]
    for peer in peers:
        pl.semaphore_signal(barrier, 1, device_id=peer, device_id_type=MESH)
    pl.semaphore_wait(barrier, len(peers))

    def role(first):
        sent = []

        def send(slot, src, dst, peer):
            i = SLOTS[slot]
            copy = pltpu.make_async_remote_copy(
                src_ref=src, dst_ref=dst, send_sem=send_sem.at[i], recv_sem=recv_sem.at[i],
                device_id=peer, device_id_type=MESH,
            )
            copy.start()
            sent.append(copy)

        def arrived(slot, dst):
            i = SLOTS[slot]
            pltpu.make_async_remote_copy(
                src_ref=dst, dst_ref=dst, send_sem=send_sem.at[i], recv_sem=recv_sem.at[i],
                device_id=pair, device_id_type=MESH,
            ).wait_recv()

        mine, theirs = (in_ref, ct_ref) if first else (ct_ref, in_ref)
        full, full_there = (b["u"], b["g"]) if first else (b["g"], b["u"])

        def send_near():
            for k in (2, 1, 3):
                send(("near", 0, k), mine, full.at[zh, x], at_x(k))

        def send_cross():
            for k in (2, 1, 3, 0):
                send(("cross", 0, k), theirs, full_there.at[zh, x], at_cross(k))

        def gather_wait():
            for k in (1, 2, 3):
                arrived(("near", 0, k), full.at[zh, ring(x, 4 - k)])
            for k in range(4):
                arrived(("cross", 0, k), full.at[1 - zh, ring(x, 4 - k)])

        def mm_forward(h):
            u = b["u"][h].reshape(HT, D)
            for dst, start in ((b["f_psend"], col_other), (b["f_own"], col)):
                for a, w in enumerate((b["wg"], b["wu"])):
                    for o, n in tiles(HC):
                        r = dot_nn(u, w[:, pl.ds(pl.multiple_of(start + o, 128), n)])
                        dst[h, a, :, :, o:o + n] = r.reshape(4, TB, n).astype(dst.dtype)
                if dst is b["f_psend"]:
                    send(("fpair", h), dst.at[h], b["f_precv"].at[h], pair)

        def mm_hidden(h):
            g = b["g"][h].reshape(HT, D)
            for dst, start in ((b["b_psend"], col_other), (b["b_own"], col)):
                for o, n in tiles(HC):
                    r = dot_nt(g, b["wd"][pl.ds(pl.multiple_of(start + o, 128), n), :])
                    dst[h, 0, :, :, o:o + n] = r.reshape(4, TB, n).astype(dst.dtype)
                if dst is b["b_psend"]:
                    send(("bpair", h), dst.at[h], b["b_precv"].at[h], pair)

        def pair_add(p, h):
            own, prec, ysend, yrecv = (b[p + n] for n in ("_own", "_precv", "_ysend", "_yrecv"))
            arrived((p + "pair", h), prec.at[h])
            for k in (2, 1, 3):
                j = ring(y, k)
                for a in range(own.shape[1]):
                    ysend[h, k - 1, a] = (own[h, a, j] + prec[h, a, j].astype(F32)).astype(BF16)
                send((p + "y", h, k), ysend.at[h, k - 1], yrecv.at[h, k - 1], at_y(k))

        def y_sum(p, h):
            own, prec, yrecv = (b[p + n] for n in ("_own", "_precv", "_yrecv"))
            total = [own[h, a, y] + prec[h, a, y].astype(F32) for a in range(own.shape[1])]
            for k in (1, 3, 2):
                arrived((p + "y", h, k), yrecv.at[h, k - 1])
            for k in (1, 2, 3):
                total = [v + yrecv[h, k - 1, a].astype(F32) for a, v in enumerate(total)]
            return total

        def block(name, h, j, start):
            ref = b[name]
            cols = pl.ds(start, HC)
            return ref.at[h, j, :, :, cols] if len(ref.shape) == 5 else ref.at[h, j, :, cols]

        def spread(name, h):
            ref = block(name, h, y, col)
            for k in (2, 1, 3):
                send((name + "y", h, k), ref, ref, at_y(k))
            send((name + "p", h, 0), ref, ref, pair)

        def forward_pair(name, h):
            for k in (1, 3, 2):
                ref = block(name, h, ring(y, 4 - k), col)
                arrived((name + "y", h, k), ref)
                send((name + "p", h, k), ref, ref, pair)

        def pair_wait(name, h):
            for k in (0, 1, 3, 2):
                arrived((name + "p", h, k), block(name, h, ring(y, 4 - k), col_other))

        def x_scatter(tag, h, term):
            for o, n in tiles(D):
                r = term(o, n).reshape(4, TB, n)
                b["xown"][tag, h, :, :, o:o + n] = r
                b["xsend"][tag, h, :, :, o:o + n] = r.astype(BF16)
            for k in (2, 1, 3):
                send(("x", tag, h, k), b["xsend"].at[tag, h, ring(x, k)], b["xrecv"].at[tag, h, k - 1], at_x(k))

        def x_sum(tag, h):
            for k in (1, 3, 2):
                arrived(("x", tag, h, k), b["xrecv"].at[tag, h, k - 1])
            total = b["xown"][tag, h, x]
            for k in (1, 2, 3):
                total = total + b["xrecv"][tag, h, k - 1].astype(F32)
            return total

        def down(tag, h):
            hid = b["hid"][h].reshape(HT, HID)
            x_scatter(tag, h, lambda o, n: dot_nn(hid, b["wd"][:, o:o + n]))

        def back(tag, h):
            gg = b["grad"][h, :, 0].reshape(HT, HID)
            gu = b["grad"][h, :, 1].reshape(HT, HID)
            x_scatter(tag, h, lambda o, n: dot_nt(gg, b["wg"][o:o + n, :]) + dot_nt(gu, b["wu"][o:o + n, :]))

        def to_next(tag, h, residual):
            total = x_sum(tag, h) + jnp.where(zh == h, residual[...].astype(F32), 0.0)
            b["zsend"][h] = total.astype(BF16)
            send_z(h)

        def send_z(h):
            for z in range(2):
                i = SLOTS[("z", h, 0)] + zh
                copy = pltpu.make_async_remote_copy(
                    src_ref=b["zsend"].at[h], dst_ref=b["zrecv"].at[h, zh],
                    send_sem=send_sem.at[SLOTS[("z", h, z)]], recv_sem=recv_sem.at[i],
                    device_id=at_other(z), device_id_type=MESH,
                )
                copy.start()
                sent.append(copy)

        def from_other(h, dst):
            for z in range(2):
                arrived(("z", h, z), b["zrecv"].at[h, z])
            total = b["zrecv"][h, 0].astype(F32) + b["zrecv"][h, 1].astype(F32)
            dst[h, x] = total.astype(BF16)
            for k in (2, 1, 3):
                send(("xg", h, k), dst.at[h, x], dst.at[h, x], at_x(k))

        def x_gathered(h, dst):
            for k in (1, 3, 2):
                arrived(("xg", h, k), dst.at[h, ring(x, 4 - k)])

        def finish(tag, residual, out_ref):
            for h in range(2):
                b["xown"][tag, h, x] = x_sum(tag, h)
            b["zzsend"][...] = b["xown"][tag, 1 - zh, x].astype(BF16)
            send(("zz",), b["zzsend"], b["zzrecv"], zz_peer)

        def finish_wait(tag, residual, out_ref):
            arrived(("zz",), b["zzrecv"])
            total = b["xown"][tag, zh, x] + b["zzrecv"][...].astype(F32) + residual[zh, x].astype(F32)
            out_ref[0] = total.astype(BF16)

        def weight_grad(lhs, rhs, out):
            for o, n in tiles(out.shape[1]):
                out[0, o:o + n, :] = dot_tn(lhs(o, n), rhs()).astype(BF16)

        def down_grad():
            weight_grad(
                lambda o, n: b["hid"][:, :, :, o:o + n].reshape(2 * HT, n),
                lambda: b["g"][...].reshape(2 * HT, D), od_ref,
            )

        def gate_grad(a):
            weight_grad(
                lambda o, n: b["u"][:, :, :, o:o + n].reshape(2 * HT, n),
                lambda: b["grad"][:, :, a].reshape(2 * HT, HID),
                (og_ref, ou_ref)[a],
            )

        both = range(2)
        if first:
            send_near()
            send_cross()
            full[zh, x] = in_ref[...]
            weights["wg"].wait()
            weights["wu"].wait()
            gather_wait()
            for h in both:
                mm_forward(h)
            for h in both:
                pair_add("f", h)
            for h in both:
                gate, up = y_sum("f", h)
                sig = 1.0 / (1.0 + jnp.exp(-gate))
                b["hid"][h, y, :, pl.ds(col, HC)] = (gate * sig * up).astype(BF16)
                spread("hid", h)
                b["fac"][h, y, 0, :, pl.ds(col, HC)] = (up * sig * (1.0 + gate * (1.0 - sig))).astype(BF16)
                b["fac"][h, y, 1, :, pl.ds(col, HC)] = (gate * sig).astype(BF16)
            weights["wd"].wait()
            for h in both:
                forward_pair("hid", h)
            for h in both:
                pair_wait("hid", h)
                down(0, h)
            for h in both:
                to_next(0, h, in_ref)
            for h in both:
                spread("fac", h)
            for h in both:
                forward_pair("fac", h)
            for h in both:
                pair_wait("fac", h)
            arrived(("home",), b["home"])
            so_ref[0] = b["home"][...]
            for h in both:
                from_other(h, b["g"])
            send(("home",), b["g"].at[zh, x], b["home"], same)
            for h in both:
                x_gathered(h, b["g"])
                mm_hidden(h)
            for h in both:
                pair_add("b", h)
            down_grad()
            for h in both:
                (gh,) = y_sum("b", h)
                b["gh"][h, y, :, pl.ds(col, HC)] = gh.astype(BF16)
                spread("gh", h)
            for h in both:
                forward_pair("gh", h)
            for h in both:
                pair_wait("gh", h)
                for j in range(4):
                    gh = b["gh"][h, j].astype(F32)
                    for a in range(2):
                        b["grad"][h, j, a] = (gh * b["fac"][h, j, a].astype(F32)).astype(BF16)
                back(1, h)
            gate_grad(0)
            finish(1, b["g"], ig_ref)
            gate_grad(1)
            finish_wait(1, b["g"], ig_ref)
        else:
            send_cross()
            send_near()
            full[zh, x] = ct_ref[...]
            weights["wd"].wait()
            gather_wait()
            for h in both:
                mm_hidden(h)
            for h in both:
                pair_add("b", h)
            for h in both:
                (b["ghown"][h],) = y_sum("b", h)
            weights["wg"].wait()
            weights["wu"].wait()
            for h in both:
                from_other(h, b["u"])
            send(("home",), b["u"].at[zh, x], b["home"], same)
            for h in both:
                x_gathered(h, b["u"])
                mm_forward(h)
            for h in both:
                pair_add("f", h)
            for h in both:
                gate, up = y_sum("f", h)
                sig = 1.0 / (1.0 + jnp.exp(-gate))
                gh = b["ghown"][h]
                grad_gate = gh * up * sig * (1.0 + gate * (1.0 - sig))
                b["grad"][h, y, 0, :, pl.ds(col, HC)] = grad_gate.astype(BF16)
                b["grad"][h, y, 1, :, pl.ds(col, HC)] = (gh * gate * sig).astype(BF16)
                spread("grad", h)
                b["hid"][h, y, :, pl.ds(col, HC)] = (gate * sig * up).astype(BF16)
            for h in both:
                forward_pair("grad", h)
            for h in both:
                pair_wait("grad", h)
                back(0, h)
            for h in both:
                to_next(0, h, ct_ref)
            for h in both:
                spread("hid", h)
            for h in both:
                forward_pair("hid", h)
            for h in both:
                pair_wait("hid", h)
                down(1, h)
            gate_grad(0)
            finish(1, b["u"], so_ref)
            gate_grad(1)
            down_grad()
            finish_wait(1, b["u"], so_ref)
            arrived(("home",), b["home"])
            ig_ref[0] = b["home"][...]
        for copy in sent:
            copy.wait_send()

    pl.when(s == 0)(lambda: role(True))
    pl.when(s == 1)(lambda: role(False))


def write_out(*refs):
    sems = refs[-1]
    half = len(refs) // 2
    copies = []
    for i, (src, dst) in enumerate(zip(refs[:half], refs[half:-1])):
        copies.append(pltpu.make_async_copy(src, dst, sems.at[i]))
        copies[-1].start()
    for copy in copies:
        copy.wait()


def per_device(inputs, cotangent, gate_weight, up_weight, down_weight):
    any_spec = pl.BlockSpec(memory_space=pl.ANY)
    vmem_spec = pl.BlockSpec(memory_space=pltpu.VMEM)
    n = len(SLOTS)
    shapes = [(1, TB, D), (1, TB, D), (1, D, HID), (1, D, HID), (1, HID, D)]
    outs = pl.pallas_call(
        kernel,
        out_shape=[pltpu.VMEM(shape, BF16) for shape in shapes],
        in_specs=[vmem_spec, vmem_spec, any_spec, any_spec, any_spec],
        out_specs=[vmem_spec] * 5,
        scratch_shapes=[pltpu.VMEM(shape, dtype) for shape, dtype in BUFFERS.values()]
        + [
            pltpu.SemaphoreType.DMA((n,)),
            pltpu.SemaphoreType.DMA((n,)),
            pltpu.SemaphoreType.DMA((3,)),
        ],
        compiler_params=pltpu.CompilerParams(
            collective_id=0, has_side_effects=True, vmem_limit_bytes=46 << 20
        ),
        name="sections",
    )(inputs, cotangent, gate_weight, up_weight, down_weight)
    return pl.pallas_call(
        write_out,
        out_shape=[jax.ShapeDtypeStruct(shape, BF16) for shape in shapes],
        in_specs=[vmem_spec] * 5,
        out_specs=[any_spec] * 5,
        scratch_shapes=[pltpu.SemaphoreType.DMA((5,))],
        compiler_params=pltpu.CompilerParams(vmem_limit_bytes=2 << 20),
        name="write_out",
    )(*outs)


def solution(mesh):
    in_specs = (
        P("tensor", "dp"),
        P("tensor", "dp"),
        P("section", "dp", "tensor"),
        P("section", "dp", "tensor"),
        P("section", "tensor", "dp"),
    )
    out_specs = (
        P("section", "tensor", "dp"),
        P("section", "tensor", "dp"),
        P("section", "dp", "tensor"),
        P("section", "dp", "tensor"),
        P("section", "tensor", "dp"),
    )
    return jax.shard_map(
        per_device, mesh=mesh, in_specs=in_specs, out_specs=out_specs, check_vma=False
    )
```

```python
import jax
import jax.numpy as jnp
from jax import lax
from jax.experimental import pallas as pl
from jax.experimental.pallas import tpu as pltpu
from jax.sharding import PartitionSpec as P

MESH = pl.DeviceIdType.MESH
F32 = jnp.float32
BF16 = jnp.bfloat16

D = 1024
HID = 1792
HC = HID // 2
NQ = 3
RB = 16
TB = 2 * RB
HT = 4 * TB

BUFFERS = {
    "wg": ((D, HID), BF16),
    "wu": ((D, HID), BF16),
    "wd": ((HID, D), BF16),
    "wgt": ((HID, D), BF16),
    "wut": ((HID, D), BF16),
    "wdt": ((D, HID), BF16),
    "u": ((NQ, 4, 2, RB, D), BF16),
    "g": ((NQ, 4, 2, RB, D), BF16),
    "hid": ((NQ, 4, TB, HID), BF16),
    "grad": ((NQ, 4, 2, TB, HID), BF16),
    "fac": ((NQ, 4, 2, TB, HID), BF16),
    "gh": ((NQ, 4, TB, HID), BF16),
    "f_psend": ((NQ, 2, 4, TB, HC), BF16),
    "f_precv": ((NQ, 2, 4, TB, HC), BF16),
    "f_own": ((NQ, 2, 4, TB, HC), F32),
    "f_ysend": ((NQ, 3, 2, TB, HC), BF16),
    "f_yrecv": ((NQ, 3, 2, TB, HC), BF16),
    "b_psend": ((NQ, 1, 4, TB, HC), BF16),
    "b_precv": ((NQ, 1, 4, TB, HC), BF16),
    "b_own": ((NQ, 1, 4, TB, HC), F32),
    "b_ysend": ((NQ, 3, 1, TB, HC), BF16),
    "b_yrecv": ((NQ, 3, 1, TB, HC), BF16),
    "ghown": ((NQ, TB, HC), F32),
    "xsend": ((2, NQ, 4, 2, RB, D), BF16),
    "xrecv": ((2, NQ, 2, 4, RB, D), BF16),
    "res": ((NQ, RB, D), BF16),
    "home": ((NQ, RB, D), BF16),
}


def slot_table():
    names = []
    for h in range(NQ):
        names += [(p, h, z, k) for p in ("in", "next") for z in range(2) for k in range(4)]
        for p in ("f", "b"):
            names.append((p + "pair", h))
            names += [(p + "y", h, k) for k in (1, 2, 3)]
        for a in ("hid", "grad", "fac", "gh"):
            names += [(a + "y", h, k) for k in (1, 2, 3)]
            names += [(a + "p", h, k) for k in range(4)]
        names += [("x", tag, h, z, k) for tag in range(2) for z in range(2) for k in range(4)]
    names += [("home",)]
    return {name: i for i, name in enumerate(names)}


SLOTS = slot_table()

ALL = [(1, 2), (1, 1), (1, 3), (0, 2), (0, 1), (0, 3), (1, 0), (0, 0)]
OTHERS = ALL[:-1]


def tiles(total, width=256):
    return [(o, min(width, total - o)) for o in range(0, total, width)]


def dot_nn(a, b):
    return lax.dot_general(a, b, (((1,), (0,)), ((), ())), preferred_element_type=F32)


def dot_nt(a, b):
    return lax.dot_general(a, b, (((1,), (1,)), ((), ())), preferred_element_type=F32)


def dot_tn(a, b):
    return lax.dot_general(a, b, (((0,), (0,)), ((), ())), preferred_element_type=F32)


def kernel(in_hbm, ct_hbm, wg_hbm, wu_hbm, wd_hbm, so_ref, ig_ref, og_ref, ou_ref, od_ref, *scratch):
    b = dict(zip(BUFFERS, scratch))
    send_sem, recv_sem, load_sem, go_sem = scratch[len(BUFFERS):]
    s, d, t = lax.axis_index("section"), lax.axis_index("dp"), lax.axis_index("tensor")
    y, c = d // 2, d % 2
    zh, x = t // 4, t % 4

    def ring(v, k):
        return (v + k) % 4

    def at_y(k):
        return {"dp": ring(y, k) * 2 + c}

    def z_hi(z):
        return zh if z == 0 else 1 - zh

    def at_x(z, k):
        return {"tensor": z_hi(z) * 4 + ring(x, k)}

    def at_next(z, k):
        return {"section": 1 - s, "tensor": z_hi(z) * 4 + ring(x, k)}

    pair = {"dp": y * 2 + 1 - c}
    same = {"section": 1 - s}
    col = pl.multiple_of(c * HC, 128)
    col_other = pl.multiple_of((1 - c) * HC, 128)

    barrier = pltpu.get_barrier_semaphore()
    peers = [pair] + [at_y(k) for k in (1, 2, 3)]
    peers += [at_x(z, k) for z, k in OTHERS] + [at_next(z, k) for z, k in ALL]
    for peer in peers:
        pl.semaphore_signal(barrier, 1, device_id=peer, device_id_type=MESH)
    weights = {}
    for i, (name, src) in enumerate((("wg", wg_hbm), ("wu", wu_hbm), ("wd", wd_hbm))):
        weights[name] = pltpu.make_async_copy(src.at[0], b[name], load_sem.at[i])
        weights[name].start()
    pl.semaphore_wait(barrier, len(peers))

    def role(first):
        sent = []
        residual = ct_hbm if first else in_hbm
        loads = []
        for h in range(NQ):
            loads.append(
                pltpu.make_async_copy(residual.at[pl.ds(h * RB, RB)], b["res"].at[h], load_sem.at[3 + h])
            )
            loads[-1].start()


        def send(slot, src, dst, peer):
            i = SLOTS[slot]
            copy = pltpu.make_async_remote_copy(
                src_ref=src, dst_ref=dst, send_sem=send_sem.at[i], recv_sem=recv_sem.at[i],
                device_id=peer, device_id_type=MESH,
            )
            copy.start()
            sent.append(copy)
            return copy

        def arrived(slot, dst):
            i = SLOTS[slot]
            pltpu.make_async_remote_copy(
                src_ref=dst, dst_ref=dst, send_sem=send_sem.at[i], recv_sem=recv_sem.at[i],
                device_id=pair, device_id_type=MESH,
            ).wait_recv()

        def gather(p, h, src, full):
            for z, k in OTHERS:
                send((p, h, z, k), src, full.at[h, x, zh], at_x(z, k))

        def gathered(p, h, full):
            for z, k in reversed(OTHERS):
                arrived((p, h, z, k), full.at[h, ring(x, 4 - k), z_hi(z)])

        def gather_input(src, full):
            for h in range(NQ):
                rows = src.at[pl.ds(h * RB, RB)]
                place = recv_sem.at[SLOTS[("in", h, 0, 0)]]
                pltpu.make_async_copy(rows, full.at[h, x, zh], place).start()
                gather("in", h, rows, full)

        def input_wait(h, full):
            arrived(("in", h, 0, 0), full.at[h, x, zh])
            gathered("in", h, full)

        def mm_forward(h):
            u = b["u"][h].reshape(HT, D)
            for dst, start in ((b["f_psend"], col_other), (b["f_own"], col)):
                for a, w in enumerate((b["wg"], b["wu"])):
                    for o, n in tiles(HC):
                        r = dot_nn(u, w[:, pl.ds(pl.multiple_of(start + o, 128), n)])
                        dst[h, a, :, :, o:o + n] = r.reshape(4, TB, n).astype(dst.dtype)
                if dst is b["f_psend"]:
                    send(("fpair", h), dst.at[h], b["f_precv"].at[h], pair)

        def mm_hidden(h):
            g = b["g"][h].reshape(HT, D)
            for dst, start in ((b["b_psend"], col_other), (b["b_own"], col)):
                for o, n in tiles(HC):
                    cols = pl.ds(pl.multiple_of(start + o, 128), n)
                    r = dot_nn(g, b["wdt"][:, cols]) if first else dot_nt(g, b["wd"][cols, :])
                    dst[h, 0, :, :, o:o + n] = r.reshape(4, TB, n).astype(dst.dtype)
                if dst is b["b_psend"]:
                    send(("bpair", h), dst.at[h], b["b_precv"].at[h], pair)

        def pair_add(p, h):
            own, prec, ysend = (b[p + n] for n in ("_own", "_precv", "_ysend"))
            arrived((p + "pair", h), prec.at[h])
            for k in (2, 1, 3):
                j = ring(y, k)
                for a in range(own.shape[1]):
                    ysend[h, k - 1, a] = (own[h, a, j] + prec[h, a, j].astype(F32)).astype(BF16)

        def y_scatter(p, h, ks=(2, 1, 3)):
            ysend, yrecv = b[p + "_ysend"], b[p + "_yrecv"]
            return [
                send((p + "y", h, k), ysend.at[h, k - 1], yrecv.at[h, k - 1], at_y(k)) for k in ks
            ]

        def y_sum(p, h):
            own, prec, yrecv = (b[p + n] for n in ("_own", "_precv", "_yrecv"))
            total = [own[h, a, y] + prec[h, a, y].astype(F32) for a in range(own.shape[1])]
            for k in (1, 3, 2):
                arrived((p + "y", h, k), yrecv.at[h, k - 1])
            for k in (1, 2, 3):
                total = [v + yrecv[h, k - 1, a].astype(F32) for a, v in enumerate(total)]
            return total

        def block(name, h, j, start):
            ref = b[name]
            cols = pl.ds(start, HC)
            return ref.at[h, j, :, :, cols] if len(ref.shape) == 5 else ref.at[h, j, :, cols]

        def spread(name, h):
            ref = block(name, h, y, col)
            copies = [send((name + "y", h, k), ref, ref, at_y(k)) for k in (2, 1, 3)]
            send((name + "p", h, 0), ref, ref, pair)
            return copies

        def forward_pair(name, h):
            for k in (1, 3, 2):
                ref = block(name, h, ring(y, 4 - k), col)
                arrived((name + "y", h, k), ref)
                send((name + "p", h, k), ref, ref, pair)

        def pair_wait(name, h):
            for k in (0, 1, 3, 2):
                arrived((name + "p", h, k), block(name, h, ring(y, 4 - k), col_other))

        def x_scatter(tag, h, term):
            for o, n in tiles(D):
                r = term(o, n).reshape(4, 2, RB, n)
                b["xsend"][tag, h, :, :, :, o:o + n] = r.astype(BF16)
            for z, k in (ALL, OTHERS)[tag]:
                send(
                    ("x", tag, h, z, k), b["xsend"].at[tag, h, ring(x, k), z_hi(z)],
                    b["xrecv"].at[tag, h, z, k], (at_next, at_x)[tag](z, k),
                )

        def x_sum(tag, h, total):
            peers = (ALL, OTHERS)[tag]
            for z, k in reversed(peers):
                arrived(("x", tag, h, z, k), b["xrecv"].at[tag, h, z, k])
            for z, k in peers:
                total = total + b["xrecv"][tag, h, z, k].astype(F32)
            return total

        def down(tag, h):
            hid = b["hid"][h].reshape(HT, HID)
            x_scatter(tag, h, lambda o, n: dot_nn(hid, b["wd"][:, o:o + n]))

        def back(tag, h):
            gg = b["grad"][h, :, 0].reshape(HT, HID)
            gu = b["grad"][h, :, 1].reshape(HT, HID)
            x_scatter(tag, h, lambda o, n: dot_nn(gg, b["wgt"][:, o:o + n]) + dot_nn(gu, b["wut"][:, o:o + n]))

        def from_other(h, dst):
            dst[h, x, zh] = x_sum(0, h, b["res"][h].astype(F32)).astype(BF16)
            gather("next", h, dst.at[h, x, zh], dst)

        def finish(h, residual, out_ref):
            total = residual[h, x, zh].astype(F32) + b["xsend"][1, h, x, zh].astype(F32)
            out_ref[0, h * RB:(h + 1) * RB] = x_sum(1, h, total).astype(BF16)

        def send_home(full):
            send(("home",), full.at[:, x, zh], b["home"], same)

        def home(out_ref):
            arrived(("home",), b["home"])
            out_ref[0] = b["home"][...].reshape(NQ * RB, D)

        def transpose(name):
            src, dst = b[name], b[name + "t"]
            for o, n in tiles(dst.shape[0]):
                dst[o:o + n, :] = src[:, o:o + n].T

        def weight_grad(lhs, rhs, out):
            for o, n in tiles(out.shape[1]):
                out[0, o:o + n, :] = dot_tn(lhs(o, n), rhs()).astype(BF16)

        def down_grad():
            weight_grad(
                lambda o, n: b["hid"][:, :, :, o:o + n].reshape(NQ * HT, n),
                lambda: b["g"][...].reshape(NQ * HT, D), od_ref,
            )

        def gate_grad(a):
            weight_grad(
                lambda o, n: b["u"][:, :, :, :, o:o + n].reshape(NQ * HT, n),
                lambda: b["grad"][:, :, a].reshape(NQ * HT, HID),
                (og_ref, ou_ref)[a],
            )

        def act_first(h):
            gate, up = y_sum("f", h)
            sig = 1.0 / (1.0 + jnp.exp(-gate))
            b["hid"][h, y, :, pl.ds(col, HC)] = (gate * sig * up).astype(BF16)
            copies = spread("hid", h)
            b["fac"][h, y, 0, :, pl.ds(col, HC)] = (up * sig * (1.0 + gate * (1.0 - sig))).astype(BF16)
            b["fac"][h, y, 1, :, pl.ds(col, HC)] = (gate * sig).astype(BF16)
            return copies

        def act_second(h):
            gate, up = y_sum("f", h)
            sig = 1.0 / (1.0 + jnp.exp(-gate))
            gh = b["ghown"][h]
            grad_gate = gh * up * sig * (1.0 + gate * (1.0 - sig))
            b["grad"][h, y, 0, :, pl.ds(col, HC)] = grad_gate.astype(BF16)
            b["grad"][h, y, 1, :, pl.ds(col, HC)] = (gh * gate * sig).astype(BF16)
            copies = spread("grad", h)
            b["hid"][h, y, :, pl.ds(col, HC)] = (gate * sig * up).astype(BF16)
            return copies

        def spread_hidden_grad(h):
            (gh,) = y_sum("b", h)
            b["gh"][h, y, :, pl.ds(col, HC)] = gh.astype(BF16)
            spread("gh", h)

        def hidden_back(tag, h):
            pair_wait("gh", h)
            for j in range(4):
                gh = b["gh"][h, j].astype(F32)
                for a in range(2):
                    b["grad"][h, j, a] = (gh * b["fac"][h, j, a].astype(F32)).astype(BF16)
            back(tag, h)

        def out_of_features(p, h):
            pair_add(p, h)
            y_scatter(p, h)

        def down_next(h):
            pair_wait("hid", h)
            down(0, h)

        def back_next(h):
            pair_wait("grad", h)
            back(0, h)

        chunks = range(NQ)

        def run(order, steps):
            for word in order:
                steps[word[0]](int(word[1]))

        if first:
            gather_input(in_hbm, b["u"])
            weights["wg"].wait()
            weights["wu"].wait()

            def start(h):
                input_wait(h, b["u"])
                mm_forward(h)

            run([
                "a0", "a1", "b0", "a2", "b1", "c0", "b2", "s0", "w0", "c1",
                "d0", "e0", "d1", "c2", "e1", "d2", "e2",
            ], {
                "a": start,
                "b": lambda h: out_of_features("f", h),
                "c": act_first,
                "d": lambda h: forward_pair("hid", h),
                "e": down_next,
                "s": lambda h: pl.semaphore_signal(go_sem, 1, device_id=same, device_id_type=MESH),
                "w": lambda h: weights["wd"].wait(),
            })
            for h in chunks:
                spread("fac", h)
            for name in ("wg", "wu", "wd"):
                transpose(name)
            for h in chunks:
                forward_pair("fac", h)
            for h in chunks:
                pair_wait("fac", h)
            for copy in loads:
                copy.wait()
            run([
                "g0", "h0", "m0", "b0", "g1", "c0", "h1", "m1", "b1", "g2",
                "t0", "d0", "e0", "c1", "h2", "m2", "b2", "d1", "e1", "c2",
                "q0", "d2", "e2", "p0", "r0", "r1", "p1", "r2",
            ], {
                "g": lambda h: from_other(h, b["g"]),
                "h": lambda h: gathered("next", h, b["g"]),
                "m": mm_hidden,
                "b": lambda h: out_of_features("b", h),
                "c": spread_hidden_grad,
                "d": lambda h: forward_pair("gh", h),
                "e": lambda h: hidden_back(1, h),
                "t": lambda h: send_home(b["g"]),
                "q": lambda h: down_grad(),
                "p": gate_grad,
                "r": lambda h: finish(h, b["g"], ig_ref),
            })
            home(so_ref)
        else:
            weights["wg"].wait()
            weights["wu"].wait()
            transpose("wg")
            transpose("wu")
            pl.semaphore_wait(go_sem, 1)
            gather_input(ct_hbm, b["g"])
            weights["wd"].wait()
            for h in chunks:
                input_wait(h, b["g"])
                mm_hidden(h)
            for h in chunks:
                out_of_features("b", h)
            for h in chunks:
                (b["ghown"][h],) = y_sum("b", h)
            for copy in loads:
                copy.wait()
            run([
                "g0", "h0", "a0", "g1", "b0", "h1", "a1", "g2", "b1", "c0",
                "h2", "a2", "b2", "c1", "d0", "e0", "c2", "d1", "e1", "d2",
                "e2",
            ], {
                "g": lambda h: from_other(h, b["u"]),
                "h": lambda h: gathered("next", h, b["u"]),
                "a": mm_forward,
                "b": lambda h: out_of_features("f", h),
                "c": act_second,
                "d": lambda h: forward_pair("grad", h),
                "e": back_next,
            })
            send_home(b["u"])
            for h in chunks:
                spread("hid", h)
            for h in chunks:
                forward_pair("hid", h)
            for h in chunks:
                pair_wait("hid", h)
                down(1, h)
            gate_grad(0)
            gate_grad(1)
            down_grad()
            for h in chunks:
                finish(h, b["u"], so_ref)
            home(ig_ref)
        for copy in sent:
            copy.wait_send()

    pl.when(s == 0)(lambda: role(True))
    pl.when(s == 1)(lambda: role(False))


def write_out(*refs):
    sems = refs[-1]
    half = len(refs) // 2
    copies = []
    for i, (src, dst) in enumerate(zip(refs[:half], refs[half:-1])):
        copies.append(pltpu.make_async_copy(src, dst, sems.at[i]))
        copies[-1].start()
    for copy in copies:
        copy.wait()


def per_device(inputs, cotangent, gate_weight, up_weight, down_weight):
    any_spec = pl.BlockSpec(memory_space=pl.ANY)
    vmem_spec = pl.BlockSpec(memory_space=pltpu.VMEM)
    n = len(SLOTS)
    shapes = [(1, NQ * RB, D), (1, NQ * RB, D), (1, D, HID), (1, D, HID), (1, HID, D)]
    outs = pl.pallas_call(
        kernel,
        out_shape=[pltpu.VMEM(shape, BF16) for shape in shapes],
        in_specs=[any_spec] * 5,
        out_specs=[vmem_spec] * 5,
        scratch_shapes=[pltpu.VMEM(shape, dtype) for shape, dtype in BUFFERS.values()]
        + [
            pltpu.SemaphoreType.DMA((n,)),
            pltpu.SemaphoreType.DMA((n,)),
            pltpu.SemaphoreType.DMA((3 + NQ,)),
            pltpu.SemaphoreType.REGULAR,
        ],
        compiler_params=pltpu.CompilerParams(
            collective_id=0, has_side_effects=True, vmem_limit_bytes=50 << 20
        ),
        name="sections",
    )(inputs, cotangent, gate_weight, up_weight, down_weight)
    return pl.pallas_call(
        write_out,
        out_shape=[jax.ShapeDtypeStruct(shape, BF16) for shape in shapes],
        in_specs=[vmem_spec] * 5,
        out_specs=[any_spec] * 5,
        scratch_shapes=[pltpu.SemaphoreType.DMA((5,))],
        compiler_params=pltpu.CompilerParams(vmem_limit_bytes=2 << 20),
        name="write_out",
    )(*outs)


def solution(mesh):
    in_specs = (
        P("tensor", "dp"),
        P("tensor", "dp"),
        P("section", "dp", "tensor"),
        P("section", "dp", "tensor"),
        P("section", "tensor", "dp"),
    )
    out_specs = (
        P("section", "tensor", "dp"),
        P("section", "tensor", "dp"),
        P("section", "dp", "tensor"),
        P("section", "dp", "tensor"),
        P("section", "tensor", "dp"),
    )
    return jax.shard_map(
        per_device, mesh=mesh, in_specs=in_specs, out_specs=out_specs, check_vma=False
    )
```

```python
import jax
import jax.numpy as jnp
from jax import lax
from jax.experimental import pallas as pl
from jax.experimental.pallas import tpu as pltpu
from jax.sharding import PartitionSpec as P

MESH = pl.DeviceIdType.MESH
F32 = jnp.float32
BF16 = jnp.bfloat16

D = 1024
HID = 1792
HC = HID // 2
NQ = 3
RB = 16
TB = 2 * RB
HT = 4 * TB

BUFFERS = {
    "wg": ((D, HID), BF16),
    "wu": ((D, HID), BF16),
    "wd": ((HID, D), BF16),
    "wgt": ((HID, D), BF16),
    "wut": ((HID, D), BF16),
    "wdt": ((D, HID), BF16),
    "u": ((NQ, 4, 2, RB, D), BF16),
    "g": ((NQ, 4, 2, RB, D), BF16),
    "hid": ((NQ, 4, TB, HID), BF16),
    "grad": ((NQ, 4, 2, TB, HID), BF16),
    "fac": ((NQ, 4, 2, TB, HID), BF16),
    "gh": ((NQ, 4, TB, HID), BF16),
    "f_psend": ((NQ, 2, 4, TB, HC), BF16),
    "f_precv": ((NQ, 2, 4, TB, HC), BF16),
    "f_own": ((NQ, 2, 4, TB, HC), F32),
    "f_ysend": ((NQ, 3, 2, TB, HC), BF16),
    "f_yrecv": ((NQ, 3, 2, TB, HC), BF16),
    "b_psend": ((NQ, 1, 4, TB, HC), BF16),
    "b_precv": ((NQ, 1, 4, TB, HC), BF16),
    "b_own": ((NQ, 1, 4, TB, HC), F32),
    "b_ysend": ((NQ, 3, 1, TB, HC), BF16),
    "b_yrecv": ((NQ, 3, 1, TB, HC), BF16),
    "ghown": ((NQ, TB, HC), F32),
    "xsend": ((2, NQ, 4, 2, RB, D), BF16),
    "xrecv": ((2, NQ, 2, 4, RB, D), BF16),
    "res": ((NQ, RB, D), BF16),
    "home": ((NQ, RB, D), BF16),
}


def slot_table():
    names = []
    for h in range(NQ):
        names += [(p, h, z, k) for p in ("in", "next") for z in range(2) for k in range(4)]
        for p in ("f", "b"):
            names.append((p + "pair", h))
            names += [(p + "y", h, k) for k in (1, 2, 3)]
        for a in ("hid", "grad", "fac", "gh"):
            names += [(a + "y", h, k) for k in (1, 2, 3)]
            names += [(a + "p", h, k) for k in range(4)]
        names += [("x", tag, h, z, k) for tag in range(2) for z in range(2) for k in range(4)]
    names += [("home",)]
    return {name: i for i, name in enumerate(names)}


SLOTS = slot_table()

ALL = [(1, 2), (1, 1), (1, 3), (0, 2), (0, 1), (0, 3), (1, 0), (0, 0)]
OTHERS = ALL[:-1]


def each_tile(total, body, width=256, unroll=False):
    if unroll:
        for o in range(0, total, width):
            body(o, min(width, total - o))
        return

    def step(i, carry):
        body(pl.multiple_of(i * width, width), width)
        return carry

    lax.fori_loop(0, total // width, step, 0)
    if total % width:
        body(total - total % width, total % width)


def dot_nn(a, b):
    return lax.dot_general(a, b, (((1,), (0,)), ((), ())), preferred_element_type=F32)


def dot_nt(a, b):
    return lax.dot_general(a, b, (((1,), (1,)), ((), ())), preferred_element_type=F32)


def dot_tn(a, b):
    return lax.dot_general(a, b, (((0,), (0,)), ((), ())), preferred_element_type=F32)


def kernel(in_hbm, ct_hbm, wg_hbm, wu_hbm, wd_hbm, so_ref, ig_ref, og_ref, ou_ref, od_ref, *scratch):
    b = dict(zip(BUFFERS, scratch))
    send_sem, recv_sem, load_sem, go_sem = scratch[len(BUFFERS):]
    s, d, t = lax.axis_index("section"), lax.axis_index("dp"), lax.axis_index("tensor")
    y, c = d // 2, d % 2
    zh, x = t // 4, t % 4

    def ring(v, k):
        return (v + k) % 4

    def at_y(k):
        return {"dp": ring(y, k) * 2 + c}

    def z_hi(z):
        return zh if z == 0 else 1 - zh

    def at_x(z, k):
        return {"tensor": z_hi(z) * 4 + ring(x, k)}

    def at_next(z, k):
        return {"section": 1 - s, "tensor": z_hi(z) * 4 + ring(x, k)}

    pair = {"dp": y * 2 + 1 - c}
    same = {"section": 1 - s}
    col = pl.multiple_of(c * HC, 128)
    col_other = pl.multiple_of((1 - c) * HC, 128)

    barrier = pltpu.get_barrier_semaphore()
    peers = [pair] + [at_y(k) for k in (1, 2, 3)]
    peers += [at_x(z, k) for z, k in OTHERS] + [at_next(z, k) for z, k in ALL]
    for peer in peers:
        pl.semaphore_signal(barrier, 1, device_id=peer, device_id_type=MESH)
    weights = {}
    for i, (name, src) in enumerate((("wg", wg_hbm), ("wu", wu_hbm), ("wd", wd_hbm))):
        weights[name] = pltpu.make_async_copy(src.at[0], b[name], load_sem.at[i])
        weights[name].start()
    pl.semaphore_wait(barrier, len(peers))

    def role(first):
        sent = []
        residual = ct_hbm if first else in_hbm
        loads = []
        for h in range(NQ):
            loads.append(
                pltpu.make_async_copy(residual.at[pl.ds(h * RB, RB)], b["res"].at[h], load_sem.at[3 + h])
            )
            loads[-1].start()


        def send(slot, src, dst, peer):
            i = SLOTS[slot]
            copy = pltpu.make_async_remote_copy(
                src_ref=src, dst_ref=dst, send_sem=send_sem.at[i], recv_sem=recv_sem.at[i],
                device_id=peer, device_id_type=MESH,
            )
            copy.start()
            sent.append(copy)
            return copy

        def arrived(slot, dst):
            i = SLOTS[slot]
            pltpu.make_async_remote_copy(
                src_ref=dst, dst_ref=dst, send_sem=send_sem.at[i], recv_sem=recv_sem.at[i],
                device_id=pair, device_id_type=MESH,
            ).wait_recv()

        def gather(p, h, src, full):
            for z, k in OTHERS:
                send((p, h, z, k), src, full.at[h, x, zh], at_x(z, k))

        def gathered(p, h, full):
            for z, k in reversed(OTHERS):
                arrived((p, h, z, k), full.at[h, ring(x, 4 - k), z_hi(z)])

        def gather_input(src, full):
            for h in range(NQ):
                rows = src.at[pl.ds(h * RB, RB)]
                place = recv_sem.at[SLOTS[("in", h, 0, 0)]]
                pltpu.make_async_copy(rows, full.at[h, x, zh], place).start()
                gather("in", h, rows, full)

        def input_wait(h, full):
            arrived(("in", h, 0, 0), full.at[h, x, zh])
            gathered("in", h, full)

        def mm_forward(h):
            u = b["u"][h].reshape(HT, D)
            for dst, start in ((b["f_psend"], col_other), (b["f_own"], col)):
                def tile(o, n):
                    for a, w in enumerate((b["wg"], b["wu"])):
                        r = dot_nn(u, w[:, pl.ds(pl.multiple_of(start + o, 128), n)])
                        dst[h, a, :, :, pl.ds(o, n)] = r.reshape(4, TB, n).astype(dst.dtype)

                each_tile(HC, tile, unroll=True)
                if dst is b["f_psend"]:
                    send(("fpair", h), dst.at[h], b["f_precv"].at[h], pair)

        def mm_hidden(h):
            g = b["g"][h].reshape(HT, D)
            for dst, start in ((b["b_psend"], col_other), (b["b_own"], col)):
                def tile(o, n):
                    cols = pl.ds(pl.multiple_of(start + o, 128), n)
                    r = dot_nn(g, b["wdt"][:, cols]) if first else dot_nt(g, b["wd"][cols, :])
                    dst[h, 0, :, :, pl.ds(o, n)] = r.reshape(4, TB, n).astype(dst.dtype)

                each_tile(HC, tile, unroll=first)
                if dst is b["b_psend"]:
                    send(("bpair", h), dst.at[h], b["b_precv"].at[h], pair)

        def pair_add(p, h):
            own, prec, ysend = (b[p + n] for n in ("_own", "_precv", "_ysend"))
            arrived((p + "pair", h), prec.at[h])
            for k in (2, 1, 3):
                j = ring(y, k)
                for a in range(own.shape[1]):
                    ysend[h, k - 1, a] = (own[h, a, j] + prec[h, a, j].astype(F32)).astype(BF16)

        def y_scatter(p, h, ks=(2, 1, 3)):
            ysend, yrecv = b[p + "_ysend"], b[p + "_yrecv"]
            return [
                send((p + "y", h, k), ysend.at[h, k - 1], yrecv.at[h, k - 1], at_y(k)) for k in ks
            ]

        def y_sum(p, h):
            own, prec, yrecv = (b[p + n] for n in ("_own", "_precv", "_yrecv"))
            total = [own[h, a, y] + prec[h, a, y].astype(F32) for a in range(own.shape[1])]
            for k in (1, 3, 2):
                arrived((p + "y", h, k), yrecv.at[h, k - 1])
            for k in (1, 2, 3):
                total = [v + yrecv[h, k - 1, a].astype(F32) for a, v in enumerate(total)]
            return total

        def block(name, h, j, start):
            ref = b[name]
            cols = pl.ds(start, HC)
            return ref.at[h, j, :, :, cols] if len(ref.shape) == 5 else ref.at[h, j, :, cols]

        def spread(name, h):
            ref = block(name, h, y, col)
            copies = [send((name + "y", h, k), ref, ref, at_y(k)) for k in (2, 1, 3)]
            send((name + "p", h, 0), ref, ref, pair)
            return copies

        def forward_pair(name, h):
            for k in (1, 3, 2):
                ref = block(name, h, ring(y, 4 - k), col)
                arrived((name + "y", h, k), ref)
                send((name + "p", h, k), ref, ref, pair)

        def pair_wait(name, h):
            for k in (0, 1, 3, 2):
                arrived((name + "p", h, k), block(name, h, ring(y, 4 - k), col_other))

        def x_scatter(tag, h, term):
            def tile(o, n):
                r = term(pl.ds(o, n)).reshape(4, 2, RB, n)
                b["xsend"][tag, h, :, :, :, pl.ds(o, n)] = r.astype(BF16)

            each_tile(D, tile, unroll=first or tag == 0)
            for z, k in (ALL, OTHERS)[tag]:
                send(
                    ("x", tag, h, z, k), b["xsend"].at[tag, h, ring(x, k), z_hi(z)],
                    b["xrecv"].at[tag, h, z, k], (at_next, at_x)[tag](z, k),
                )

        def x_sum(tag, h, total):
            peers = (ALL, OTHERS)[tag]
            for z, k in reversed(peers):
                arrived(("x", tag, h, z, k), b["xrecv"].at[tag, h, z, k])
            for z, k in peers:
                total = total + b["xrecv"][tag, h, z, k].astype(F32)
            return total

        def down(tag, h):
            hid = b["hid"][h].reshape(HT, HID)
            x_scatter(tag, h, lambda cols: dot_nn(hid, b["wd"][:, cols]))

        def back(tag, h):
            gg = b["grad"][h, :, 0].reshape(HT, HID)
            gu = b["grad"][h, :, 1].reshape(HT, HID)
            x_scatter(tag, h, lambda cols: dot_nn(gg, b["wgt"][:, cols]) + dot_nn(gu, b["wut"][:, cols]))

        def from_other(h, dst):
            dst[h, x, zh] = x_sum(0, h, b["res"][h].astype(F32)).astype(BF16)
            gather("next", h, dst.at[h, x, zh], dst)

        def finish(h, residual, out_ref):
            total = residual[h, x, zh].astype(F32) + b["xsend"][1, h, x, zh].astype(F32)
            out_ref[0, h * RB:(h + 1) * RB] = x_sum(1, h, total).astype(BF16)

        def send_home(full):
            send(("home",), full.at[:, x, zh], b["home"], same)

        def home(out_ref):
            arrived(("home",), b["home"])
            out_ref[0] = b["home"][...].reshape(NQ * RB, D)

        def transpose(name):
            src, dst = b[name], b[name + "t"]
            def tile(o, n):
                dst[pl.ds(o, n), :] = src[:, pl.ds(o, n)].T

            each_tile(dst.shape[0], tile)

        def weight_grad(lhs, rhs, out):
            def tile(o, n):
                out[0, pl.ds(o, n), :] = dot_tn(lhs(o, n), rhs()).astype(BF16)

            each_tile(out.shape[1], tile)

        def down_grad():
            weight_grad(
                lambda o, n: b["hid"][:, :, :, pl.ds(o, n)].reshape(NQ * HT, n),
                lambda: b["g"][...].reshape(NQ * HT, D), od_ref,
            )

        def gate_grad(a):
            weight_grad(
                lambda o, n: b["u"][:, :, :, :, pl.ds(o, n)].reshape(NQ * HT, n),
                lambda: b["grad"][:, :, a].reshape(NQ * HT, HID),
                (og_ref, ou_ref)[a],
            )

        def act_first(h):
            gate, up = y_sum("f", h)
            sig = 1.0 / (1.0 + jnp.exp(-gate))
            b["hid"][h, y, :, pl.ds(col, HC)] = (gate * sig * up).astype(BF16)
            copies = spread("hid", h)
            b["fac"][h, y, 0, :, pl.ds(col, HC)] = (up * sig * (1.0 + gate * (1.0 - sig))).astype(BF16)
            b["fac"][h, y, 1, :, pl.ds(col, HC)] = (gate * sig).astype(BF16)
            return copies

        def act_second(h):
            gate, up = y_sum("f", h)
            sig = 1.0 / (1.0 + jnp.exp(-gate))
            gh = b["ghown"][h]
            grad_gate = gh * up * sig * (1.0 + gate * (1.0 - sig))
            b["grad"][h, y, 0, :, pl.ds(col, HC)] = grad_gate.astype(BF16)
            b["grad"][h, y, 1, :, pl.ds(col, HC)] = (gh * gate * sig).astype(BF16)
            copies = spread("grad", h)
            b["hid"][h, y, :, pl.ds(col, HC)] = (gate * sig * up).astype(BF16)
            return copies

        def spread_hidden_grad(h):
            (gh,) = y_sum("b", h)
            b["gh"][h, y, :, pl.ds(col, HC)] = gh.astype(BF16)
            spread("gh", h)

        def hidden_back(tag, h):
            pair_wait("gh", h)
            for j in range(4):
                gh = b["gh"][h, j].astype(F32)
                for a in range(2):
                    b["grad"][h, j, a] = (gh * b["fac"][h, j, a].astype(F32)).astype(BF16)
            back(tag, h)

        def out_of_features(p, h):
            pair_add(p, h)
            y_scatter(p, h)

        def down_next(h):
            pair_wait("hid", h)
            down(0, h)

        def back_next(h):
            pair_wait("grad", h)
            back(0, h)

        chunks = range(NQ)

        def run(order, steps):
            for word in order:
                steps[word[0]](int(word[1]))

        if first:
            gather_input(in_hbm, b["u"])
            weights["wg"].wait()
            weights["wu"].wait()

            def start(h):
                input_wait(h, b["u"])
                mm_forward(h)

            run([
                "a0", "a1", "b0", "a2", "b1", "c0", "b2", "s0", "w0", "c1",
                "d0", "e0", "d1", "c2", "e1", "d2", "e2",
            ], {
                "a": start,
                "b": lambda h: out_of_features("f", h),
                "c": act_first,
                "d": lambda h: forward_pair("hid", h),
                "e": down_next,
                "s": lambda h: pl.semaphore_signal(go_sem, 1, device_id=same, device_id_type=MESH),
                "w": lambda h: weights["wd"].wait(),
            })
            for h in chunks:
                spread("fac", h)
            for name in ("wg", "wu", "wd"):
                transpose(name)
            for h in chunks:
                forward_pair("fac", h)
            for h in chunks:
                pair_wait("fac", h)
            for copy in loads:
                copy.wait()
            run([
                "g0", "h0", "m0", "b0", "g1", "c0", "h1", "m1", "b1", "g2",
                "t0", "d0", "e0", "c1", "h2", "m2", "b2", "d1", "e1", "c2",
                "q0", "d2", "e2", "p0", "r0", "r1", "p1", "r2",
            ], {
                "g": lambda h: from_other(h, b["g"]),
                "h": lambda h: gathered("next", h, b["g"]),
                "m": mm_hidden,
                "b": lambda h: out_of_features("b", h),
                "c": spread_hidden_grad,
                "d": lambda h: forward_pair("gh", h),
                "e": lambda h: hidden_back(1, h),
                "t": lambda h: send_home(b["g"]),
                "q": lambda h: down_grad(),
                "p": gate_grad,
                "r": lambda h: finish(h, b["g"], ig_ref),
            })
            home(so_ref)
        else:
            weights["wg"].wait()
            weights["wu"].wait()
            transpose("wg")
            transpose("wu")
            pl.semaphore_wait(go_sem, 1)
            gather_input(ct_hbm, b["g"])
            weights["wd"].wait()
            for h in chunks:
                input_wait(h, b["g"])
                mm_hidden(h)
            for h in chunks:
                out_of_features("b", h)
            for h in chunks:
                (b["ghown"][h],) = y_sum("b", h)
            for copy in loads:
                copy.wait()
            run([
                "g0", "h0", "a0", "g1", "b0", "h1", "a1", "g2", "b1", "c0",
                "h2", "a2", "b2", "c1", "d0", "e0", "c2", "d1", "e1", "d2",
                "e2",
            ], {
                "g": lambda h: from_other(h, b["u"]),
                "h": lambda h: gathered("next", h, b["u"]),
                "a": mm_forward,
                "b": lambda h: out_of_features("f", h),
                "c": act_second,
                "d": lambda h: forward_pair("grad", h),
                "e": back_next,
            })
            send_home(b["u"])
            for h in chunks:
                spread("hid", h)
            for h in chunks:
                forward_pair("hid", h)
            for h in chunks:
                pair_wait("hid", h)
                down(1, h)
            gate_grad(0)
            gate_grad(1)
            down_grad()
            for h in chunks:
                finish(h, b["u"], so_ref)
            home(ig_ref)
        for copy in sent:
            copy.wait_send()

    pl.when(s == 0)(lambda: role(True))
    pl.when(s == 1)(lambda: role(False))


def write_out(*refs):
    sems = refs[-1]
    half = len(refs) // 2
    copies = []
    for src, dst in zip(refs[:half], refs[half:-1]):
        rows = src.shape[1]
        step = rows if rows < 1024 else rows // 4
        for o in range(0, rows, step):
            part = pl.ds(o, step)
            copies.append(pltpu.make_async_copy(src.at[:, part], dst.at[:, part], sems.at[len(copies)]))
            copies[-1].start()
    for copy in copies:
        copy.wait()


def per_device(inputs, cotangent, gate_weight, up_weight, down_weight):
    any_spec = pl.BlockSpec(memory_space=pl.ANY)
    vmem_spec = pl.BlockSpec(memory_space=pltpu.VMEM)
    n = len(SLOTS)
    shapes = [(1, NQ * RB, D), (1, NQ * RB, D), (1, D, HID), (1, D, HID), (1, HID, D)]
    outs = pl.pallas_call(
        kernel,
        out_shape=[pltpu.VMEM(shape, BF16) for shape in shapes],
        in_specs=[any_spec] * 5,
        out_specs=[vmem_spec] * 5,
        scratch_shapes=[pltpu.VMEM(shape, dtype) for shape, dtype in BUFFERS.values()]
        + [
            pltpu.SemaphoreType.DMA((n,)),
            pltpu.SemaphoreType.DMA((n,)),
            pltpu.SemaphoreType.DMA((3 + NQ,)),
            pltpu.SemaphoreType.REGULAR,
        ],
        compiler_params=pltpu.CompilerParams(
            collective_id=0, has_side_effects=True, vmem_limit_bytes=50 << 20
        ),
        name="sections",
    )(inputs, cotangent, gate_weight, up_weight, down_weight)
    return pl.pallas_call(
        write_out,
        out_shape=[jax.ShapeDtypeStruct(shape, BF16) for shape in shapes],
        in_specs=[vmem_spec] * 5,
        out_specs=[any_spec] * 5,
        scratch_shapes=[pltpu.SemaphoreType.DMA((14,))],
        compiler_params=pltpu.CompilerParams(vmem_limit_bytes=2 << 20),
        name="write_out",
    )(*outs)


def solution(mesh):
    in_specs = (
        P("tensor", "dp"),
        P("tensor", "dp"),
        P("section", "dp", "tensor"),
        P("section", "dp", "tensor"),
        P("section", "tensor", "dp"),
    )
    out_specs = (
        P("section", "tensor", "dp"),
        P("section", "tensor", "dp"),
        P("section", "dp", "tensor"),
        P("section", "dp", "tensor"),
        P("section", "tensor", "dp"),
    )
    return jax.shard_map(
        per_device, mesh=mesh, in_specs=in_specs, out_specs=out_specs, check_vma=False
    )
```

```python
import jax
import jax.numpy as jnp
from jax import lax
from jax.experimental import pallas as pl
from jax.experimental.pallas import tpu as pltpu
from jax.sharding import PartitionSpec as P

MESH = pl.DeviceIdType.MESH
F32 = jnp.float32
BF16 = jnp.bfloat16

D = 1024
HID = 1792
HC = HID // 2
NQ = 3
RB = 16
TB = 2 * RB
HT = 4 * TB

BUFFERS = {
    "wg": ((D, HID), BF16),
    "wu": ((D, HID), BF16),
    "wd": ((HID, D), BF16),
    "wgt": ((HID, D), BF16),
    "wut": ((HID, D), BF16),
    "wdt": ((D, HID), BF16),
    "u": ((NQ, 4, 2, RB, D), BF16),
    "g": ((NQ, 4, 2, RB, D), BF16),
    "hid": ((NQ, 4, TB, HID), BF16),
    "grad": ((NQ, 4, 2, TB, HID), BF16),
    "fac": ((NQ, 4, 2, TB, HID), BF16),
    "gh": ((NQ, 4, TB, HID), BF16),
    "f_psend": ((NQ, 2, 4, TB, HC), BF16),
    "f_precv": ((NQ, 2, 4, TB, HC), BF16),
    "f_own": ((NQ, 2, 4, TB, HC), F32),
    "f_ysend": ((NQ, 3, 2, TB, HC), BF16),
    "f_yrecv": ((NQ, 3, 2, TB, HC), BF16),
    "b_psend": ((NQ, 1, 4, TB, HC), BF16),
    "b_precv": ((NQ, 1, 4, TB, HC), BF16),
    "b_own": ((NQ, 1, 4, TB, HC), F32),
    "b_ysend": ((NQ, 3, 1, TB, HC), BF16),
    "b_yrecv": ((NQ, 3, 1, TB, HC), BF16),
    "xsend": ((2, NQ, 4, 2, RB, D), BF16),
    "xrecv": ((2, NQ, 2, 4, RB, D), BF16),
    "res": ((NQ, RB, D), BF16),
    "acc": ((HT, D), F32),
    "home": ((NQ, RB, D), BF16),
}


def slot_table():
    names = []
    for h in range(NQ):
        names += [(p, h, z, k) for p in ("in", "next") for z in range(2) for k in range(4)]
        for p in ("f", "b"):
            names.append((p + "pair", h))
            names += [(p + "y", h, k) for k in (1, 2, 3)]
        for a in ("hid", "grad", "fac", "gh"):
            names += [(a + "y", h, k) for k in (1, 2, 3)]
            names += [(a + "p", h, k) for k in range(4)]
        names += [
            ("x", tag, h, z, k, part)
            for tag in range(2) for z in range(2) for k in range(4) for part in range(2)
        ]
    names += [("home",)]
    return {name: i for i, name in enumerate(names)}


SLOTS = slot_table()

ALL = [(1, 2), (1, 1), (1, 3), (0, 2), (0, 1), (0, 3), (1, 0), (0, 0)]
OTHERS = ALL[:-1]


def each_tile(total, body, width=256, unroll=False):
    if unroll:
        for o in range(0, total, width):
            body(o, min(width, total - o))
        return

    def step(i, carry):
        body(pl.multiple_of(i * width, width), width)
        return carry

    lax.fori_loop(0, total // width, step, 0)
    if total % width:
        body(total - total % width, total % width)


def dot_nn(a, b):
    return lax.dot_general(a, b, (((1,), (0,)), ((), ())), preferred_element_type=F32)


def dot_nt(a, b):
    return lax.dot_general(a, b, (((1,), (1,)), ((), ())), preferred_element_type=F32)


def dot_tn(a, b):
    return lax.dot_general(a, b, (((0,), (0,)), ((), ())), preferred_element_type=F32)


def kernel(in_hbm, ct_hbm, wg_hbm, wu_hbm, wd_hbm, so_ref, ig_ref, og_ref, ou_ref, od_ref, *scratch):
    b = dict(zip(BUFFERS, scratch))
    send_sem, recv_sem, load_sem, go_sem = scratch[len(BUFFERS):]
    s, d, t = lax.axis_index("section"), lax.axis_index("dp"), lax.axis_index("tensor")
    y, c = d // 2, d % 2
    zh, x = t // 4, t % 4

    def ring(v, k):
        return (v + k) % 4

    def at_y(k):
        return {"dp": ring(y, k) * 2 + c}

    def z_hi(z):
        return zh if z == 0 else 1 - zh

    def at_x(z, k):
        return {"tensor": z_hi(z) * 4 + ring(x, k)}

    def at_next(z, k):
        return {"section": 1 - s, "tensor": z_hi(z) * 4 + ring(x, k)}

    pair = {"dp": y * 2 + 1 - c}
    same = {"section": 1 - s}
    col = pl.multiple_of(c * HC, 128)
    col_other = pl.multiple_of((1 - c) * HC, 128)

    barrier = pltpu.get_barrier_semaphore()
    peers = [pair] + [at_y(k) for k in (1, 2, 3)]
    peers += [at_x(z, k) for z, k in OTHERS] + [at_next(z, k) for z, k in ALL]
    for peer in peers:
        pl.semaphore_signal(barrier, 1, device_id=peer, device_id_type=MESH)
    weights = {}
    for i, (name, src) in enumerate((("wg", wg_hbm), ("wu", wu_hbm), ("wd", wd_hbm))):
        weights[name] = pltpu.make_async_copy(src.at[0], b[name], load_sem.at[i])
        weights[name].start()
    pl.semaphore_wait(barrier, len(peers))

    def role(first):
        sent = []
        residual = ct_hbm if first else in_hbm
        loads = []
        for h in range(NQ):
            loads.append(
                pltpu.make_async_copy(residual.at[pl.ds(h * RB, RB)], b["res"].at[h], load_sem.at[3 + h])
            )
            loads[-1].start()


        def send(slot, src, dst, peer):
            i = SLOTS[slot]
            copy = pltpu.make_async_remote_copy(
                src_ref=src, dst_ref=dst, send_sem=send_sem.at[i], recv_sem=recv_sem.at[i],
                device_id=peer, device_id_type=MESH,
            )
            copy.start()
            sent.append(copy)
            return copy

        def arrived(slot, dst):
            i = SLOTS[slot]
            pltpu.make_async_remote_copy(
                src_ref=dst, dst_ref=dst, send_sem=send_sem.at[i], recv_sem=recv_sem.at[i],
                device_id=pair, device_id_type=MESH,
            ).wait_recv()

        def gather(p, h, src, full):
            for z, k in OTHERS:
                send((p, h, z, k), src, full.at[h, x, zh], at_x(z, k))

        def gathered(p, h, full):
            for z, k in reversed(OTHERS):
                arrived((p, h, z, k), full.at[h, ring(x, 4 - k), z_hi(z)])

        def gather_input(src, full):
            for h in range(NQ):
                rows = src.at[pl.ds(h * RB, RB)]
                place = recv_sem.at[SLOTS[("in", h, 0, 0)]]
                pltpu.make_async_copy(rows, full.at[h, x, zh], place).start()
                gather("in", h, rows, full)

        def input_wait(h, full):
            arrived(("in", h, 0, 0), full.at[h, x, zh])
            gathered("in", h, full)

        def mm_forward(h):
            u = b["u"][h].reshape(HT, D)
            for dst, start in ((b["f_psend"], col_other), (b["f_own"], col)):
                def tile(o, n):
                    for a, w in enumerate((b["wg"], b["wu"])):
                        r = dot_nn(u, w[:, pl.ds(pl.multiple_of(start + o, 128), n)])
                        dst[h, a, :, :, pl.ds(o, n)] = r.reshape(4, TB, n).astype(dst.dtype)

                each_tile(HC, tile, unroll=True)
                if dst is b["f_psend"]:
                    send(("fpair", h), dst.at[h], b["f_precv"].at[h], pair)

        def mm_hidden(h):
            g = b["g"][h].reshape(HT, D)
            for dst, start in ((b["b_psend"], col_other), (b["b_own"], col)):
                def tile(o, n):
                    cols = pl.ds(pl.multiple_of(start + o, 128), n)
                    r = dot_nn(g, b["wdt"][:, cols]) if first else dot_nt(g, b["wd"][cols, :])
                    dst[h, 0, :, :, pl.ds(o, n)] = r.reshape(4, TB, n).astype(dst.dtype)

                each_tile(HC, tile, unroll=first)
                if dst is b["b_psend"]:
                    send(("bpair", h), dst.at[h], b["b_precv"].at[h], pair)

        def out_of_features(p, h):
            own, prec, ysend, yrecv = (b[p + n] for n in ("_own", "_precv", "_ysend", "_yrecv"))
            arrived((p + "pair", h), prec.at[h])
            for k in (2, 1, 3):
                j = ring(y, k)
                for a in range(own.shape[1]):
                    ysend[h, k - 1, a] = (own[h, a, j] + prec[h, a, j].astype(F32)).astype(BF16)
                send((p + "y", h, k), ysend.at[h, k - 1], yrecv.at[h, k - 1], at_y(k))

        def y_sum(p, h):
            own, prec, yrecv = (b[p + n] for n in ("_own", "_precv", "_yrecv"))
            total = [own[h, a, y] + prec[h, a, y].astype(F32) for a in range(own.shape[1])]
            for k in (1, 3, 2):
                arrived((p + "y", h, k), yrecv.at[h, k - 1])
            for k in (1, 2, 3):
                total = [v + yrecv[h, k - 1, a].astype(F32) for a, v in enumerate(total)]
            return total

        def block(name, h, j, start):
            ref = b[name]
            cols = pl.ds(start, HC)
            return ref.at[h, j, :, :, cols] if len(ref.shape) == 5 else ref.at[h, j, :, cols]

        def spread(name, h):
            ref = block(name, h, y, col)
            copies = [send((name + "y", h, k), ref, ref, at_y(k)) for k in (2, 1, 3)]
            send((name + "p", h, 0), ref, ref, pair)
            return copies

        def forward_pair(name, h):
            for k in (1, 3, 2):
                ref = block(name, h, ring(y, 4 - k), col)
                arrived((name + "y", h, k), ref)
                send((name + "p", h, k), ref, ref, pair)

        def pair_wait(name, h):
            for k in (0, 1, 3, 2):
                arrived((name + "p", h, k), block(name, h, ring(y, 4 - k), col_other))

        def x_scatter(tag, h, term):
            def tile(o, n):
                r = term(pl.ds(o, n)).reshape(4, 2, RB, n)
                b["xsend"][tag, h, :, :, :, pl.ds(o, n)] = r.astype(BF16)

            for part in range(2):
                start = part * (D // 2)
                each_tile(D // 2, lambda o, n: tile(start + o, n), unroll=first or tag == 0)
                cols = pl.ds(start, D // 2)
                for z, k in (ALL, OTHERS)[tag]:
                    send(
                        ("x", tag, h, z, k, part), b["xsend"].at[tag, h, ring(x, k), z_hi(z), :, cols],
                        b["xrecv"].at[tag, h, z, k, :, cols], (at_next, at_x)[tag](z, k),
                    )

        def x_sum(tag, h, total):
            peers = (ALL, OTHERS)[tag]
            for part in range(2):
                cols = pl.ds(part * (D // 2), D // 2)
                for z, k in reversed(peers):
                    arrived(("x", tag, h, z, k, part), b["xrecv"].at[tag, h, z, k, :, cols])
            for z, k in peers:
                total = total + b["xrecv"][tag, h, z, k].astype(F32)
            return total

        def over_hidden(tag, h, name, term):
            own, other = pl.ds(col, HC), pl.ds(col_other, HC)

            def tile(o, n):
                b["acc"][:, pl.ds(o, n)] = term(own, pl.ds(o, n))

            each_tile(D, tile, unroll=first or tag == 0)
            pair_wait(name, h)
            return lambda cols: b["acc"][:, cols] + term(other, cols)

        def down(tag, h):
            x_scatter(tag, h, over_hidden(tag, h, "hid", lambda part, cols: dot_nn(
                b["hid"][h, :, :, part].reshape(HT, HC), b["wd"][part, cols]
            )))

        def back(tag, h, name):
            def term(part, cols):
                gg = b["grad"][h, :, 0, :, part].reshape(HT, HC)
                gu = b["grad"][h, :, 1, :, part].reshape(HT, HC)
                return dot_nn(gg, b["wgt"][part, cols]) + dot_nn(gu, b["wut"][part, cols])

            later = over_hidden(tag, h, name, term)
            if first:
                hidden_grads(h, col_other)
            x_scatter(tag, h, later)

        def from_other(h, dst):
            dst[h, x, zh] = x_sum(0, h, b["res"][h].astype(F32)).astype(BF16)
            gather("next", h, dst.at[h, x, zh], dst)

        def finish(h, residual, out_ref):
            total = residual[h, x, zh].astype(F32) + b["xsend"][1, h, x, zh].astype(F32)
            out_ref[0, h * RB:(h + 1) * RB] = x_sum(1, h, total).astype(BF16)

        def send_home(full):
            send(("home",), full.at[:, x, zh], b["home"], same)

        def home(out_ref):
            arrived(("home",), b["home"])
            out_ref[0] = b["home"][...].reshape(NQ * RB, D)

        def transpose(name):
            src, dst = b[name], b[name + "t"]
            def tile(o, n):
                dst[pl.ds(o, n), :] = src[:, pl.ds(o, n)].T

            each_tile(dst.shape[0], tile)

        def weight_grad(lhs, rhs, out):
            def tile(o, n):
                out[0, pl.ds(o, n), :] = dot_tn(lhs(o, n), rhs()).astype(BF16)

            each_tile(out.shape[1], tile)

        def down_grad():
            weight_grad(
                lambda o, n: b["hid"][:, :, :, pl.ds(o, n)].reshape(NQ * HT, n),
                lambda: b["g"][...].reshape(NQ * HT, D), od_ref,
            )

        def gate_grad(a):
            weight_grad(
                lambda o, n: b["u"][:, :, :, :, pl.ds(o, n)].reshape(NQ * HT, n),
                lambda: b["grad"][:, :, a].reshape(NQ * HT, HID),
                (og_ref, ou_ref)[a],
            )

        def act_first(h):
            gate, up = y_sum("f", h)
            sig = 1.0 / (1.0 + jnp.exp(-gate))
            b["hid"][h, y, :, pl.ds(col, HC)] = (gate * sig * up).astype(BF16)
            copies = spread("hid", h)
            b["fac"][h, y, 0, :, pl.ds(col, HC)] = (up * sig * (1.0 + gate * (1.0 - sig))).astype(BF16)
            b["fac"][h, y, 1, :, pl.ds(col, HC)] = (gate * sig).astype(BF16)
            return copies

        def act_second(h):
            (gh,) = y_sum("b", h)
            gate, up = y_sum("f", h)
            sig = 1.0 / (1.0 + jnp.exp(-gate))
            grad_gate = gh * up * sig * (1.0 + gate * (1.0 - sig))
            b["grad"][h, y, 0, :, pl.ds(col, HC)] = grad_gate.astype(BF16)
            b["grad"][h, y, 1, :, pl.ds(col, HC)] = (gh * gate * sig).astype(BF16)
            copies = spread("grad", h)
            b["hid"][h, y, :, pl.ds(col, HC)] = (gate * sig * up).astype(BF16)
            return copies

        def spread_hidden_grad(h):
            (gh,) = y_sum("b", h)
            b["gh"][h, y, :, pl.ds(col, HC)] = gh.astype(BF16)
            spread("gh", h)

        def hidden_grads(h, start):
            cols = pl.ds(start, HC)
            for j in range(4):
                gh = b["gh"][h, j, :, cols].astype(F32)
                for a in range(2):
                    b["grad"][h, j, a, :, cols] = (gh * b["fac"][h, j, a, :, cols].astype(F32)).astype(BF16)

        def hidden_back(tag, h):
            hidden_grads(h, col)
            back(tag, h, "gh")

        chunks = range(NQ)

        def run(order, steps):
            for word in order:
                steps[word[0]](int(word[1]))

        if first:
            gather_input(in_hbm, b["u"])
            weights["wg"].wait()
            weights["wu"].wait()

            def start(h):
                input_wait(h, b["u"])
                mm_forward(h)

            run([
                "a0", "b0", "a1", "b1", "a2", "s0", "c0", "b2", "w0", "c1",
                "d0", "e0", "d1", "c2", "e1", "d2", "e2",
            ], {
                "a": start,
                "b": lambda h: out_of_features("f", h),
                "c": act_first,
                "d": lambda h: forward_pair("hid", h),
                "e": lambda h: down(0, h),
                "s": lambda h: pl.semaphore_signal(go_sem, 1, device_id=same, device_id_type=MESH),
                "w": lambda h: weights["wd"].wait(),
            })
            for h in chunks:
                spread("fac", h)
            for name in ("wg", "wu", "wd"):
                transpose(name)
            for h in chunks:
                forward_pair("fac", h)
            for h in chunks:
                pair_wait("fac", h)
            for copy in loads:
                copy.wait()
            run([
                "g0", "h0", "m0", "b0", "g1", "c0", "h1", "m1", "b1", "g2",
                "t0", "d0", "e0", "c1", "h2", "m2", "b2", "d1", "e1", "c2",
                "q0", "d2", "e2", "p0", "r0", "r1", "p1", "r2",
            ], {
                "g": lambda h: from_other(h, b["g"]),
                "h": lambda h: gathered("next", h, b["g"]),
                "m": mm_hidden,
                "b": lambda h: out_of_features("b", h),
                "c": spread_hidden_grad,
                "d": lambda h: forward_pair("gh", h),
                "e": lambda h: hidden_back(1, h),
                "t": lambda h: send_home(b["g"]),
                "q": lambda h: down_grad(),
                "p": gate_grad,
                "r": lambda h: finish(h, b["g"], ig_ref),
            })
            home(so_ref)
        else:
            weights["wg"].wait()
            weights["wu"].wait()
            transpose("wg")
            transpose("wu")
            pl.semaphore_wait(go_sem, 1)
            gather_input(ct_hbm, b["g"])
            weights["wd"].wait()
            for h in chunks:
                input_wait(h, b["g"])
                mm_hidden(h)
            for h in chunks:
                out_of_features("b", h)
            for copy in loads:
                copy.wait()
            run([
                "g0", "h0", "a0", "g1", "b0", "h1", "a1", "g2", "b1", "c0",
                "h2", "a2", "b2", "c1", "d0", "e0", "c2", "d1", "e1", "d2",
                "e2",
            ], {
                "g": lambda h: from_other(h, b["u"]),
                "h": lambda h: gathered("next", h, b["u"]),
                "a": mm_forward,
                "b": lambda h: out_of_features("f", h),
                "c": act_second,
                "d": lambda h: forward_pair("grad", h),
                "e": lambda h: back(0, h, "grad"),
            })
            send_home(b["u"])
            for h in chunks:
                spread("hid", h)
            for h in chunks:
                forward_pair("hid", h)
            for h in chunks:
                down(1, h)
            gate_grad(0)
            gate_grad(1)
            down_grad()
            for h in chunks:
                finish(h, b["u"], so_ref)
            home(ig_ref)
        for copy in sent:
            copy.wait_send()

    pl.when(s == 0)(lambda: role(True))
    pl.when(s == 1)(lambda: role(False))


def write_out(*refs):
    sems = refs[-1]
    half = len(refs) // 2
    copies = []
    for src, dst in zip(refs[:half], refs[half:-1]):
        rows = src.shape[1]
        step = rows if rows < 1024 else rows // 4
        for o in range(0, rows, step):
            part = pl.ds(o, step)
            copies.append(pltpu.make_async_copy(src.at[:, part], dst.at[:, part], sems.at[len(copies)]))
            copies[-1].start()
    for copy in copies:
        copy.wait()


def per_device(inputs, cotangent, gate_weight, up_weight, down_weight):
    any_spec = pl.BlockSpec(memory_space=pl.ANY)
    vmem_spec = pl.BlockSpec(memory_space=pltpu.VMEM)
    n = len(SLOTS)
    shapes = [(1, NQ * RB, D), (1, NQ * RB, D), (1, D, HID), (1, D, HID), (1, HID, D)]
    outs = pl.pallas_call(
        kernel,
        out_shape=[pltpu.VMEM(shape, BF16) for shape in shapes],
        in_specs=[any_spec] * 5,
        out_specs=[vmem_spec] * 5,
        scratch_shapes=[pltpu.VMEM(shape, dtype) for shape, dtype in BUFFERS.values()]
        + [
            pltpu.SemaphoreType.DMA((n,)),
            pltpu.SemaphoreType.DMA((n,)),
            pltpu.SemaphoreType.DMA((3 + NQ,)),
            pltpu.SemaphoreType.REGULAR,
        ],
        compiler_params=pltpu.CompilerParams(
            collective_id=0, has_side_effects=True, vmem_limit_bytes=50 << 20
        ),
        name="sections",
    )(inputs, cotangent, gate_weight, up_weight, down_weight)
    return pl.pallas_call(
        write_out,
        out_shape=[jax.ShapeDtypeStruct(shape, BF16) for shape in shapes],
        in_specs=[vmem_spec] * 5,
        out_specs=[any_spec] * 5,
        scratch_shapes=[pltpu.SemaphoreType.DMA((14,))],
        compiler_params=pltpu.CompilerParams(vmem_limit_bytes=2 << 20),
        name="write_out",
    )(*outs)


def solution(mesh):
    in_specs = (
        P("tensor", "dp"),
        P("tensor", "dp"),
        P("section", "dp", "tensor"),
        P("section", "dp", "tensor"),
        P("section", "tensor", "dp"),
    )
    out_specs = (
        P("section", "tensor", "dp"),
        P("section", "tensor", "dp"),
        P("section", "dp", "tensor"),
        P("section", "dp", "tensor"),
        P("section", "tensor", "dp"),
    )
    return jax.shard_map(
        per_device, mesh=mesh, in_specs=in_specs, out_specs=out_specs, check_vma=False
    )
```

```python
import jax
import jax.numpy as jnp
from jax import lax
from jax.experimental import pallas as pl
from jax.experimental.pallas import tpu as pltpu
from jax.sharding import PartitionSpec as P

MESH = pl.DeviceIdType.MESH
F32 = jnp.float32
BF16 = jnp.bfloat16

D = 1024
HID = 1792
HC = HID // 2
NQ = 3
RB = 16
TB = 2 * RB
HT = 4 * TB

BUFFERS = {
    "wg": ((D, HID), BF16),
    "wu": ((D, HID), BF16),
    "wd": ((HID, D), BF16),
    "wgt": ((HID, D), BF16),
    "wut": ((HID, D), BF16),
    "wdt": ((D, HID), BF16),
    "u": ((NQ, 4, 2, RB, D), BF16),
    "g": ((NQ, 4, 2, RB, D), BF16),
    "hid": ((NQ, 4, TB, HID), BF16),
    "grad": ((NQ, 4, 2, TB, HID), BF16),
    "fac": ((NQ, 4, 2, TB, HID), BF16),
    "gh": ((NQ, 4, TB, HID), BF16),
    "f_psend": ((NQ, 2, 4, TB, HC), BF16),
    "f_precv": ((NQ, 2, 4, TB, HC), BF16),
    "f_own": ((NQ, 2, 4, TB, HC), F32),
    "f_ysend": ((NQ, 3, 2, TB, HC), BF16),
    "f_yrecv": ((NQ, 3, 2, TB, HC), BF16),
    "b_psend": ((NQ, 1, 4, TB, HC), BF16),
    "b_precv": ((NQ, 1, 4, TB, HC), BF16),
    "b_own": ((NQ, 1, 4, TB, HC), F32),
    "b_ysend": ((NQ, 3, 1, TB, HC), BF16),
    "b_yrecv": ((NQ, 3, 1, TB, HC), BF16),
    "xsend": ((2, NQ, 4, 2, RB, D), BF16),
    "xrecv": ((2, NQ, 2, 4, RB, D), BF16),
    "res": ((NQ, RB, D), BF16),
    "acc": ((HT, D), F32),
    "home": ((NQ, RB, D), BF16),
}


def slot_table():
    names = []
    for h in range(NQ):
        names += [("in", h, z, k) for z in range(2) for k in range(4)]
        names += [("next", h, z, k, part) for z in range(2) for k in range(4) for part in range(2)]
        for p in ("f", "b"):
            names.append((p + "pair", h))
            names += [(p + "y", h, k) for k in (1, 2, 3)]
        for a in ("hid", "grad", "fac", "gh"):
            names += [(a + "y", h, k) for k in (1, 2, 3)]
            names += [(a + "p", h, k) for k in range(4)]
        names += [
            ("x", tag, h, z, k, part)
            for tag in range(2) for z in range(2) for k in range(4) for part in range(2)
        ]
    names += [("home",)]
    return {name: i for i, name in enumerate(names)}


SLOTS = slot_table()

ALL = [(1, 2), (1, 1), (1, 3), (0, 2), (0, 1), (0, 3), (1, 0), (0, 0)]
OTHERS = ALL[:-1]


def each_tile(total, body, width=256, unroll=False):
    if unroll:
        for o in range(0, total, width):
            body(o, min(width, total - o))
        return

    def step(i, carry):
        body(pl.multiple_of(i * width, width), width)
        return carry

    lax.fori_loop(0, total // width, step, 0)
    if total % width:
        body(total - total % width, total % width)


def dot_nn(a, b):
    return lax.dot_general(a, b, (((1,), (0,)), ((), ())), preferred_element_type=F32)


def dot_nt(a, b):
    return lax.dot_general(a, b, (((1,), (1,)), ((), ())), preferred_element_type=F32)


def dot_tn(a, b):
    return lax.dot_general(a, b, (((0,), (0,)), ((), ())), preferred_element_type=F32)


def kernel(in_hbm, ct_hbm, wg_hbm, wu_hbm, wd_hbm, so_ref, ig_ref, og_ref, ou_ref, od_ref, *scratch):
    b = dict(zip(BUFFERS, scratch))
    send_sem, recv_sem, load_sem, go_sem = scratch[len(BUFFERS):]
    s, d, t = lax.axis_index("section"), lax.axis_index("dp"), lax.axis_index("tensor")
    y, c = d // 2, d % 2
    zh, x = t // 4, t % 4

    def ring(v, k):
        return (v + k) % 4

    def at_y(k):
        return {"dp": ring(y, k) * 2 + c}

    def z_hi(z):
        return zh if z == 0 else 1 - zh

    def at_x(z, k):
        return {"tensor": z_hi(z) * 4 + ring(x, k)}

    def at_next(z, k):
        return {"section": 1 - s, "tensor": z_hi(z) * 4 + ring(x, k)}

    pair = {"dp": y * 2 + 1 - c}
    same = {"section": 1 - s}
    col = pl.multiple_of(c * HC, 128)
    col_other = pl.multiple_of((1 - c) * HC, 128)

    barrier = pltpu.get_barrier_semaphore()
    peers = [pair] + [at_y(k) for k in (1, 2, 3)]
    peers += [at_x(z, k) for z, k in OTHERS] + [at_next(z, k) for z, k in ALL]
    for peer in peers:
        pl.semaphore_signal(barrier, 1, device_id=peer, device_id_type=MESH)
    weights = {}
    for i, (name, src) in enumerate((("wg", wg_hbm), ("wu", wu_hbm), ("wd", wd_hbm))):
        weights[name] = pltpu.make_async_copy(src.at[0], b[name], load_sem.at[i])
        weights[name].start()
    pl.semaphore_wait(barrier, len(peers))

    def role(first):
        sent = []
        residual = ct_hbm if first else in_hbm
        loads = []
        for h in range(NQ):
            loads.append(
                pltpu.make_async_copy(residual.at[pl.ds(h * RB, RB)], b["res"].at[h], load_sem.at[3 + h])
            )
            loads[-1].start()


        def send(slot, src, dst, peer):
            i = SLOTS[slot]
            copy = pltpu.make_async_remote_copy(
                src_ref=src, dst_ref=dst, send_sem=send_sem.at[i], recv_sem=recv_sem.at[i],
                device_id=peer, device_id_type=MESH,
            )
            copy.start()
            sent.append(copy)
            return copy

        def arrived(slot, dst):
            i = SLOTS[slot]
            pltpu.make_async_remote_copy(
                src_ref=dst, dst_ref=dst, send_sem=send_sem.at[i], recv_sem=recv_sem.at[i],
                device_id=pair, device_id_type=MESH,
            ).wait_recv()

        def gather(p, h, src, full):
            for z, k in OTHERS:
                send((p, h, z, k), src, full.at[h, x, zh], at_x(z, k))

        def gathered(p, h, full):
            for z, k in reversed(OTHERS):
                arrived((p, h, z, k), full.at[h, ring(x, 4 - k), z_hi(z)])

        def gather_input(src, full):
            for h in range(NQ):
                rows = src.at[pl.ds(h * RB, RB)]
                place = recv_sem.at[SLOTS[("in", h, 0, 0)]]
                pltpu.make_async_copy(rows, full.at[h, x, zh], place).start()
                gather("in", h, rows, full)

        def input_wait(h, full):
            arrived(("in", h, 0, 0), full.at[h, x, zh])
            gathered("in", h, full)

        def mm_forward(h):
            u = b["u"][h].reshape(HT, D)
            for dst, start in ((b["f_psend"], col_other), (b["f_own"], col)):
                def tile(o, n):
                    for a, w in enumerate((b["wg"], b["wu"])):
                        r = dot_nn(u, w[:, pl.ds(pl.multiple_of(start + o, 128), n)])
                        dst[h, a, :, :, pl.ds(o, n)] = r.reshape(4, TB, n).astype(dst.dtype)

                each_tile(HC, tile, unroll=True)
                if dst is b["f_psend"]:
                    send(("fpair", h), dst.at[h], b["f_precv"].at[h], pair)

        def mm_hidden(h):
            g = b["g"][h].reshape(HT, D)
            for dst, start in ((b["b_psend"], col_other), (b["b_own"], col)):
                def tile(o, n):
                    cols = pl.ds(pl.multiple_of(start + o, 128), n)
                    r = dot_nn(g, b["wdt"][:, cols]) if first else dot_nt(g, b["wd"][cols, :])
                    dst[h, 0, :, :, pl.ds(o, n)] = r.reshape(4, TB, n).astype(dst.dtype)

                each_tile(HC, tile, unroll=first)
                if dst is b["b_psend"]:
                    send(("bpair", h), dst.at[h], b["b_precv"].at[h], pair)

        def out_of_features(p, h):
            own, prec, ysend, yrecv = (b[p + n] for n in ("_own", "_precv", "_ysend", "_yrecv"))
            arrived((p + "pair", h), prec.at[h])
            for k in (2, 1, 3):
                j = ring(y, k)
                for a in range(own.shape[1]):
                    ysend[h, k - 1, a] = (own[h, a, j] + prec[h, a, j].astype(F32)).astype(BF16)
                send((p + "y", h, k), ysend.at[h, k - 1], yrecv.at[h, k - 1], at_y(k))

        def y_sum(p, h):
            own, prec, yrecv = (b[p + n] for n in ("_own", "_precv", "_yrecv"))
            total = [own[h, a, y] + prec[h, a, y].astype(F32) for a in range(own.shape[1])]
            for k in (1, 3, 2):
                arrived((p + "y", h, k), yrecv.at[h, k - 1])
            for k in (1, 2, 3):
                total = [v + yrecv[h, k - 1, a].astype(F32) for a, v in enumerate(total)]
            return total

        def block(name, h, j, start):
            ref = b[name]
            cols = pl.ds(start, HC)
            return ref.at[h, j, :, :, cols] if len(ref.shape) == 5 else ref.at[h, j, :, cols]

        def spread(name, h):
            ref = block(name, h, y, col)
            copies = [send((name + "y", h, k), ref, ref, at_y(k)) for k in (2, 1, 3)]
            send((name + "p", h, 0), ref, ref, pair)
            return copies

        def forward_pair(name, h):
            for k in (1, 3, 2):
                ref = block(name, h, ring(y, 4 - k), col)
                arrived((name + "y", h, k), ref)
                send((name + "p", h, k), ref, ref, pair)

        def pair_wait(name, h):
            for k in (0, 1, 3, 2):
                arrived((name + "p", h, k), block(name, h, ring(y, 4 - k), col_other))

        def x_scatter(tag, h, term):
            def tile(o, n):
                r = term(pl.ds(o, n)).reshape(4, 2, RB, n)
                b["xsend"][tag, h, :, :, :, pl.ds(o, n)] = r.astype(BF16)

            for part in range(2):
                start = part * (D // 2)
                each_tile(D // 2, lambda o, n: tile(start + o, n), unroll=first or tag == 0)
                cols = pl.ds(start, D // 2)
                for z, k in (ALL, OTHERS)[tag]:
                    send(
                        ("x", tag, h, z, k, part), b["xsend"].at[tag, h, ring(x, k), z_hi(z), :, cols],
                        b["xrecv"].at[tag, h, z, k, :, cols], (at_next, at_x)[tag](z, k),
                    )

        def x_sum(tag, h, total, part):
            peers = (ALL, OTHERS)[tag]
            cols = pl.ds(part * (D // 2), D // 2)
            for z, k in reversed(peers):
                arrived(("x", tag, h, z, k, part), b["xrecv"].at[tag, h, z, k, :, cols])
            for z, k in peers:
                total = total + b["xrecv"][tag, h, z, k, :, cols].astype(F32)
            return total

        def over_hidden(tag, h, name, term):
            own, other = pl.ds(col, HC), pl.ds(col_other, HC)

            def tile(o, n):
                b["acc"][:, pl.ds(o, n)] = term(own, pl.ds(o, n))

            each_tile(D, tile, unroll=first or tag == 0)
            pair_wait(name, h)
            return lambda cols: b["acc"][:, cols] + term(other, cols)

        def down(tag, h):
            x_scatter(tag, h, over_hidden(tag, h, "hid", lambda part, cols: dot_nn(
                b["hid"][h, :, :, part].reshape(HT, HC), b["wd"][part, cols]
            )))

        def back(tag, h, name):
            def term(part, cols):
                gg = b["grad"][h, :, 0, :, part].reshape(HT, HC)
                gu = b["grad"][h, :, 1, :, part].reshape(HT, HC)
                return dot_nn(gg, b["wgt"][part, cols]) + dot_nn(gu, b["wut"][part, cols])

            later = over_hidden(tag, h, name, term)
            if first:
                hidden_grads(h, col_other)
            x_scatter(tag, h, later)

        def from_other(h, dst):
            for part in range(2):
                cols = pl.ds(part * (D // 2), D // 2)
                own = dst.at[h, x, zh, :, cols]
                own[...] = x_sum(0, h, b["res"][h, :, cols].astype(F32), part).astype(BF16)
                for z, k in OTHERS:
                    send(("next", h, z, k, part), own, own, at_x(z, k))

        def next_wait(h, full):
            for part in range(2):
                cols = pl.ds(part * (D // 2), D // 2)
                for z, k in reversed(OTHERS):
                    arrived(("next", h, z, k, part), full.at[h, ring(x, 4 - k), z_hi(z), :, cols])

        def finish(h, residual, out_ref):
            for part in range(2):
                cols = pl.ds(part * (D // 2), D // 2)
                total = residual[h, x, zh, :, cols].astype(F32) + b["xsend"][1, h, x, zh, :, cols].astype(F32)
                out_ref[0, h * RB:(h + 1) * RB, cols] = x_sum(1, h, total, part).astype(BF16)

        def send_home(full):
            send(("home",), full.at[:, x, zh], b["home"], same)

        def home(out_ref):
            arrived(("home",), b["home"])
            out_ref[0] = b["home"][...].reshape(NQ * RB, D)

        def transpose(name):
            src, dst = b[name], b[name + "t"]
            def tile(o, n):
                dst[pl.ds(o, n), :] = src[:, pl.ds(o, n)].T

            each_tile(dst.shape[0], tile)

        def weight_grad(lhs, rhs, out):
            def tile(o, n):
                out[0, pl.ds(o, n), :] = dot_tn(lhs(o, n), rhs()).astype(BF16)

            each_tile(out.shape[1], tile)

        def down_grad():
            weight_grad(
                lambda o, n: b["hid"][:, :, :, pl.ds(o, n)].reshape(NQ * HT, n),
                lambda: b["g"][...].reshape(NQ * HT, D), od_ref,
            )

        def gate_grad(a):
            weight_grad(
                lambda o, n: b["u"][:, :, :, :, pl.ds(o, n)].reshape(NQ * HT, n),
                lambda: b["grad"][:, :, a].reshape(NQ * HT, HID),
                (og_ref, ou_ref)[a],
            )

        def act_first(h):
            gate, up = y_sum("f", h)
            sig = 1.0 / (1.0 + jnp.exp(-gate))
            b["hid"][h, y, :, pl.ds(col, HC)] = (gate * sig * up).astype(BF16)
            copies = spread("hid", h)
            b["fac"][h, y, 0, :, pl.ds(col, HC)] = (up * sig * (1.0 + gate * (1.0 - sig))).astype(BF16)
            b["fac"][h, y, 1, :, pl.ds(col, HC)] = (gate * sig).astype(BF16)
            return copies

        def act_second(h):
            (gh,) = y_sum("b", h)
            gate, up = y_sum("f", h)
            sig = 1.0 / (1.0 + jnp.exp(-gate))
            grad_gate = gh * up * sig * (1.0 + gate * (1.0 - sig))
            b["grad"][h, y, 0, :, pl.ds(col, HC)] = grad_gate.astype(BF16)
            b["grad"][h, y, 1, :, pl.ds(col, HC)] = (gh * gate * sig).astype(BF16)
            copies = spread("grad", h)
            b["hid"][h, y, :, pl.ds(col, HC)] = (gate * sig * up).astype(BF16)
            return copies

        def spread_hidden_grad(h):
            (gh,) = y_sum("b", h)
            b["gh"][h, y, :, pl.ds(col, HC)] = gh.astype(BF16)
            spread("gh", h)

        def hidden_grads(h, start):
            cols = pl.ds(start, HC)
            for j in range(4):
                gh = b["gh"][h, j, :, cols].astype(F32)
                for a in range(2):
                    b["grad"][h, j, a, :, cols] = (gh * b["fac"][h, j, a, :, cols].astype(F32)).astype(BF16)

        def hidden_back(tag, h):
            hidden_grads(h, col)
            back(tag, h, "gh")

        chunks = range(NQ)

        def run(order, steps):
            for word in order:
                steps[word[0]](int(word[1]))

        if first:
            gather_input(in_hbm, b["u"])
            weights["wg"].wait()
            weights["wu"].wait()

            def start(h):
                input_wait(h, b["u"])
                mm_forward(h)

            run([
                "a0", "b0", "a1", "b1", "a2", "s0", "c0", "b2", "w0", "c1",
                "d0", "e0", "d1", "c2", "e1", "d2", "e2",
            ], {
                "a": start,
                "b": lambda h: out_of_features("f", h),
                "c": act_first,
                "d": lambda h: forward_pair("hid", h),
                "e": lambda h: down(0, h),
                "s": lambda h: pl.semaphore_signal(go_sem, 1, device_id=same, device_id_type=MESH),
                "w": lambda h: weights["wd"].wait(),
            })
            for h in chunks:
                spread("fac", h)
            for name in ("wg", "wu", "wd"):
                transpose(name)
            for h in chunks:
                forward_pair("fac", h)
            for h in chunks:
                pair_wait("fac", h)
            for copy in loads:
                copy.wait()
            run([
                "g0", "h0", "m0", "b0", "g1", "c0", "h1", "m1", "b1", "g2",
                "t0", "d0", "e0", "c1", "h2", "m2", "b2", "d1", "e1", "c2",
                "q0", "d2", "e2", "p0", "r0", "r1", "p1", "r2",
            ], {
                "g": lambda h: from_other(h, b["g"]),
                "h": lambda h: next_wait(h, b["g"]),
                "m": mm_hidden,
                "b": lambda h: out_of_features("b", h),
                "c": spread_hidden_grad,
                "d": lambda h: forward_pair("gh", h),
                "e": lambda h: hidden_back(1, h),
                "t": lambda h: send_home(b["g"]),
                "q": lambda h: down_grad(),
                "p": gate_grad,
                "r": lambda h: finish(h, b["g"], ig_ref),
            })
            home(so_ref)
        else:
            weights["wg"].wait()
            weights["wu"].wait()
            transpose("wg")
            transpose("wu")
            pl.semaphore_wait(go_sem, 1)
            gather_input(ct_hbm, b["g"])
            weights["wd"].wait()
            for h in chunks:
                input_wait(h, b["g"])
                mm_hidden(h)
            for h in chunks:
                out_of_features("b", h)
            for copy in loads:
                copy.wait()
            run([
                "g0", "h0", "a0", "g1", "b0", "h1", "a1", "g2", "b1", "c0",
                "h2", "a2", "b2", "c1", "d0", "e0", "c2", "d1", "e1", "d2",
                "e2",
            ], {
                "g": lambda h: from_other(h, b["u"]),
                "h": lambda h: next_wait(h, b["u"]),
                "a": mm_forward,
                "b": lambda h: out_of_features("f", h),
                "c": act_second,
                "d": lambda h: forward_pair("grad", h),
                "e": lambda h: back(0, h, "grad"),
            })
            send_home(b["u"])
            for h in chunks:
                spread("hid", h)
            for h in chunks:
                forward_pair("hid", h)
            for h in chunks:
                down(1, h)
            gate_grad(0)
            gate_grad(1)
            down_grad()
            for h in chunks:
                finish(h, b["u"], so_ref)
            home(ig_ref)
        for copy in sent:
            copy.wait_send()

    pl.when(s == 0)(lambda: role(True))
    pl.when(s == 1)(lambda: role(False))


def write_out(*refs):
    sems = refs[-1]
    half = len(refs) // 2
    copies = []
    for src, dst in zip(refs[:half], refs[half:-1]):
        rows = src.shape[1]
        step = rows if rows < 1024 else rows // 4
        for o in range(0, rows, step):
            part = pl.ds(o, step)
            copies.append(pltpu.make_async_copy(src.at[:, part], dst.at[:, part], sems.at[len(copies)]))
            copies[-1].start()
    for copy in copies:
        copy.wait()


def per_device(inputs, cotangent, gate_weight, up_weight, down_weight):
    any_spec = pl.BlockSpec(memory_space=pl.ANY)
    vmem_spec = pl.BlockSpec(memory_space=pltpu.VMEM)
    n = len(SLOTS)
    shapes = [(1, NQ * RB, D), (1, NQ * RB, D), (1, D, HID), (1, D, HID), (1, HID, D)]
    outs = pl.pallas_call(
        kernel,
        out_shape=[pltpu.VMEM(shape, BF16) for shape in shapes],
        in_specs=[any_spec] * 5,
        out_specs=[vmem_spec] * 5,
        scratch_shapes=[pltpu.VMEM(shape, dtype) for shape, dtype in BUFFERS.values()]
        + [
            pltpu.SemaphoreType.DMA((n,)),
            pltpu.SemaphoreType.DMA((n,)),
            pltpu.SemaphoreType.DMA((3 + NQ,)),
            pltpu.SemaphoreType.REGULAR,
        ],
        compiler_params=pltpu.CompilerParams(
            collective_id=0, has_side_effects=True, vmem_limit_bytes=50 << 20
        ),
        name="sections",
    )(inputs, cotangent, gate_weight, up_weight, down_weight)
    return pl.pallas_call(
        write_out,
        out_shape=[jax.ShapeDtypeStruct(shape, BF16) for shape in shapes],
        in_specs=[vmem_spec] * 5,
        out_specs=[any_spec] * 5,
        scratch_shapes=[pltpu.SemaphoreType.DMA((14,))],
        compiler_params=pltpu.CompilerParams(vmem_limit_bytes=2 << 20),
        name="write_out",
    )(*outs)


def solution(mesh):
    in_specs = (
        P("tensor", "dp"),
        P("tensor", "dp"),
        P("section", "dp", "tensor"),
        P("section", "dp", "tensor"),
        P("section", "tensor", "dp"),
    )
    out_specs = (
        P("section", "tensor", "dp"),
        P("section", "tensor", "dp"),
        P("section", "dp", "tensor"),
        P("section", "dp", "tensor"),
        P("section", "tensor", "dp"),
    )
    return jax.shard_map(
        per_device, mesh=mesh, in_specs=in_specs, out_specs=out_specs, check_vma=False
    )
```
